32 devices in a mesh: ctx: 8 (over z, x), head: 4 (over y, core).
Axes of the slice: x: 2, y: 2, z: 4, core: 2. Of those that a mesh axis runs over, the one named last changes fastest.
Arguments:
- tokens: bfloat16 [4096, 7168], P(('ctx', 'head')), may hold values from -6 to 6
- routes: int32 [4096, 8], P(('ctx', 'head')), may hold values from 0 to 255, all different within a row; in each aligned block of 128 rows (0 to 127, 128 to 255, ...) at most 6 rows name the same one
- route_weight: float32 [4096, 8], P(('ctx', 'head')), may hold values from 0.2 to 2
- w_gate: bfloat16 [8, 7168, 1024], P('ctx', 'head'), may hold values from -0.0625 to 0.0625
- w_up: bfloat16 [8, 7168, 1024], P('ctx', 'head'), may hold values from -0.0625 to 0.0625
- w_down: bfloat16 [8, 1024, 7168], P('ctx', None, 'head'), may hold values from -0.1875 to 0.1875
- grad_out: bfloat16 [4096, 7168], P(('ctx', 'head')), may hold values from -6 to 6
Outputs:
- moe_out: bfloat16 [4096, 7168], P(('ctx', 'head'))
- grad_tokens: bfloat16 [4096, 7168], P(('ctx', 'head'))
- grad_route: float32 [4096, 8], P(('ctx', 'head'))
- grad_gate: bfloat16 [8, 7168, 1024], P('ctx', 'head')
- grad_up: bfloat16 [8, 7168, 1024], P('ctx', 'head')
- grad_down: bfloat16 [8, 1024, 7168], P('ctx', None, 'head')
The draws below stay inside these ranges and needn't reach their ends.
Inputs may be any that keep to these rules, and one draw needn't show every extreme that they name: `routes`: each row names 8 different experts. In each aligned block of 128 rows (the tokens of one device) no expert is named more than 6 times. Experts below 8 are the window's.
All inputs are finite; a program needn't handle non-finite values.
Results may differ from the reference program's by a relative error of at most 0.0057.
Values may be sent and summed in bfloat16 or wider, within the bound.
A program may use at most 128 MiB of HBM per device.

```python
import math
import jax
import jax.numpy as jnp
import numpy as np
from jax import lax

D = 7168
FFE = 1024
ALL_EXP = 256
TOPK = 8
TOK_DEV = 128
EXPERTS = 8
CAP = 6
TOKENS = 4096


def levels(stream_key, extent, split, low, largest):
    def one(dim, blocks):
        heights = jax.random.uniform(jax.random.fold_in(jax.random.fold_in(stream_key, 6), dim), (blocks,), jnp.float32, low / len(split), largest / len(split))
        return jnp.repeat(jnp.exp(heights), extent[dim] // blocks).reshape((-1,) + (1,) * (len(extent) - dim - 1))

    level = one(*split[0])
    for cut in split[1:]:
        level = level * one(*cut)
    return level


def assign_block(stream_key, own, number, rows, number_of, top, limit, lean):
    sequence = jax.random.permutation(stream_key, number_of)
    crowded, ordinary = load_shares(number_of, rows * top, limit, lean, True), load_shares(number_of, rows * top, limit, lean, False)
    places = jnp.arange(number_of)

    def named(tallies, offset_by):
        used = int((tallies > 0).sum())
        fixed = max(1, used // 4)
        moved = fixed + (places - fixed + offset_by * (used - fixed)) % max(1, number_of - fixed)
        return jnp.zeros((number_of,), jnp.int32).at[sequence[jnp.where(places < fixed, places, moved)]].set(jnp.asarray(tallies, jnp.int32))

    tallies = jnp.where(number % 4 == 0, named(crowded, number // 4), named(ordinary, number - number // 4 - 1))
    mixed = jax.random.permutation(jax.random.fold_in(own, 3), number_of)
    source_of, taker = mixed[0:number_of // 2 * 2:2], mixed[1:number_of // 2 * 2:2]
    slack = jnp.minimum(tallies[source_of] - 1, limit - tallies[taker]) // 2
    slack = jnp.where((source_of == sequence[0]) | (taker == sequence[0]) | (tallies[taker] == 0), 0, jnp.maximum(slack, 0))
    moved = jax.random.randint(jax.random.fold_in(own, 4), (number_of // 2,), 0, 1 << 20) % (slack + 1)
    tallies = tallies.at[source_of].add(-moved).at[taker].add(moved)
    labels = jnp.searchsorted(jnp.cumsum(tallies), jnp.arange(rows * top), side="right").astype(jnp.int32)
    grid = labels.reshape(top, rows).T
    grid = grid[jax.random.permutation(jax.random.fold_in(own, 1), rows)]
    offset_by = jax.random.randint(jax.random.fold_in(own, 2), (rows, 1), 0, top)
    return jnp.take_along_axis(grid, (jnp.arange(top)[None, :] + offset_by) % top, axis=1)


def load_shares(amount, total, bound, skew, full):
    portions = [(1 << 20) // math.isqrt(standing ** skew) + 1 for standing in range(1, amount + 1)]
    largest = bound if full else min(bound, max(-(-total // amount), total * portions[0] // sum(portions)))
    least = 1 if total - largest >= amount - 1 else 0
    counts, surplus = [largest] + [least] * (amount - 1), total - largest - least * (amount - 1)
    while surplus > 0:
        free = [i for i in range(1, amount) if counts[i] < largest] or [i for i in range(1, amount) if counts[i] < bound]
        whole, budget = sum([portions[i] for i in free]), surplus
        for i in free:
            extra = min(bound - counts[i], max(1, budget * portions[i] // whole), surplus)
            counts[i] = counts[i] + extra
            surplus = surplus - extra
    return np.array(counts)


def scatter_about(own_key, dims, deviation, reach, cuts=(), kind=jnp.bfloat16):
    gain = levels(own_key, dims, cuts, -0.22, 0.18) if cuts else 1.0
    values = jax.random.normal(own_key, dims, jnp.float32) * deviation * gain
    return jnp.minimum(jnp.maximum(values, -reach), reach).astype(kind)


def setup_inputs(seed: int = 0) -> dict:
    seeds = jax.random.split(jax.random.key(seed), 8)
    tokens = scatter_about(seeds[0], (TOKENS, D), 1.0, 6.0, ((0, 32),))
    routes_keys = jax.random.split(jax.random.fold_in(seeds[1], 1), TOKENS // TOK_DEV)
    routes_turns = jax.random.permutation(jax.random.fold_in(seeds[1], 3), TOKENS // TOK_DEV)
    routes = jax.vmap(lambda own, number: assign_block(jax.random.fold_in(seeds[1], 2), own, number, TOK_DEV, ALL_EXP, TOPK, CAP, 2))(routes_keys, routes_turns).reshape((TOKENS, TOPK))
    route_weight = jnp.clip(jnp.exp(math.log(2.0) - 2.3025851 * jax.random.uniform(seeds[2], (TOKENS, TOPK), jnp.float32) ** levels(seeds[2], (TOKENS, TOPK), ((0, 32),), -0.2, 0.2)), 0.2, 2.0)
    w_gate = scatter_about(seeds[3], (EXPERTS, D, FFE), D ** -0.5, 0.0625, ((0, 8), (1, 4)))
    w_up = scatter_about(seeds[4], (EXPERTS, D, FFE), D ** -0.5, 0.0625, ((0, 8), (1, 4)))
    w_down = scatter_about(seeds[5], (EXPERTS, FFE, D), FFE ** -0.5, 0.1875, ((0, 8), (2, 4)))
    grad_out = scatter_about(seeds[6], (TOKENS, D), 1.0, 6.0, ((0, 32),))
    return {"tokens": tokens, "routes": routes, "route_weight": route_weight, "w_gate": w_gate, "w_up": w_up, "w_down": w_down, "grad_out": grad_out}


def silu_parts(gate_pre):
    sigmoid_g = jax.nn.sigmoid(gate_pre)
    return gate_pre * sigmoid_g, sigmoid_g * (1.0 + gate_pre * (1.0 - sigmoid_g))


def reference(tokens, routes, route_weight, w_gate, w_up, w_down, grad_out):
    block_count = TOKENS // TOK_DEV
    flat_routes = routes.reshape(block_count, TOK_DEV * TOPK)
    onehot = (flat_routes[:, :, None] == jnp.arange(EXPERTS, dtype=jnp.int32)[None, None, :]).astype(jnp.int32)
    before = jnp.sum((jnp.cumsum(onehot, axis=1) - onehot) * onehot, axis=2).astype(jnp.int32)
    block_ids = jnp.arange(block_count, dtype=jnp.int32)[:, None]
    slot_rows = block_count * CAP
    slot_ids = flat_routes * slot_rows + block_ids * CAP + before
    slot_ids = jnp.where(flat_routes < EXPERTS, slot_ids, EXPERTS * slot_rows).astype(jnp.int32)
    pick_ids = jnp.arange(TOKENS * TOPK, dtype=jnp.int32)
    table = jnp.full((EXPERTS * slot_rows,), -1, jnp.int32).at[slot_ids.reshape(-1)].set(pick_ids, mode="drop")
    weights_flat = route_weight.reshape(-1)

    def per_expert(state, expert):
        out_sum, grad_sum, route_sum = state
        entry = lax.dynamic_slice_in_dim(table, expert * slot_rows, slot_rows)
        filled = entry >= 0
        pick_safe = jnp.where(filled, entry, 0).astype(jnp.int32)
        token_ids = (pick_safe // TOPK).astype(jnp.int32)
        scale = jnp.where(filled, weights_flat[pick_safe], jnp.zeros((), jnp.float32))
        x_rows = jnp.where(filled[:, None], tokens[token_ids], jnp.zeros((), jnp.bfloat16))
        dy_rows = jnp.where(filled[:, None], grad_out[token_ids], jnp.zeros((), jnp.bfloat16)).astype(jnp.float32)
        do_rows = (scale[:, None] * dy_rows).astype(jnp.bfloat16)
        gate_w = w_gate[expert]
        up_w = w_up[expert]
        down_w = w_down[expert]
        gate_pre = jnp.dot(x_rows, gate_w, preferred_element_type=jnp.float32)
        up_value = jnp.dot(x_rows, up_w, preferred_element_type=jnp.float32)
        back_grad = jnp.dot(do_rows, down_w.T, preferred_element_type=jnp.float32)
        smooth, silu_slope = silu_parts(gate_pre)
        hidden = (smooth * up_value).astype(jnp.bfloat16)
        d_gate = (back_grad * up_value * silu_slope).astype(jnp.bfloat16)
        d_up = (back_grad * smooth).astype(jnp.bfloat16)
        expert_out = jnp.dot(hidden, down_w, preferred_element_type=jnp.float32).astype(jnp.bfloat16)
        grad_rows = (jnp.dot(d_gate, gate_w.T, preferred_element_type=jnp.float32)
                     + jnp.dot(d_up, up_w.T, preferred_element_type=jnp.float32)).astype(jnp.bfloat16)
        grad_gate = jnp.dot(x_rows.T, d_gate, preferred_element_type=jnp.float32).astype(jnp.bfloat16)
        grad_up = jnp.dot(x_rows.T, d_up, preferred_element_type=jnp.float32).astype(jnp.bfloat16)
        grad_down = jnp.dot(hidden.T, do_rows, preferred_element_type=jnp.float32).astype(jnp.bfloat16)
        targets = jnp.where(filled, token_ids, TOKENS).astype(jnp.int32)
        out_float = expert_out.astype(jnp.float32)
        out_sum = out_sum.at[targets].add(scale[:, None] * out_float, mode="drop")
        grad_sum = grad_sum.at[targets].add(grad_rows.astype(jnp.float32), mode="drop")
        pick_target = jnp.where(filled, entry, TOKENS * TOPK).astype(jnp.int32)
        route_sum = route_sum.at[pick_target].add(jnp.sum(dy_rows * out_float, axis=1), mode="drop")
        return (out_sum, grad_sum, route_sum), (grad_gate, grad_up, grad_down)

    initial = (jnp.zeros((TOKENS, D), jnp.float32), jnp.zeros((TOKENS, D), jnp.float32),
               jnp.zeros((TOKENS * TOPK,), jnp.float32))
    totals, weight_grads = lax.scan(per_expert, initial, jnp.arange(EXPERTS, dtype=jnp.int32))
    out_sum, grad_sum, route_sum = totals
    grad_gate, grad_up, grad_down = weight_grads
    return (out_sum.astype(jnp.bfloat16), grad_sum.astype(jnp.bfloat16), route_sum.reshape(TOKENS, TOPK),
            grad_gate, grad_up, grad_down)
```

```python
import functools

import jax
import jax.numpy as jnp
from jax import lax
from jax.experimental import pallas as pl
from jax.experimental.pallas import tpu as pltpu
from jax.sharding import PartitionSpec as P

CAP = 6
PARTS = 2
SLOTS = CAP // PARTS
ROWS = 16
LANES = 128
MESH = pl.DeviceIdType.MESH
F32 = jnp.float32
BF16 = jnp.bfloat16
VMEM_BYTES = 60 * 1024 * 1024


def block_cols(slice_width):
    tiles = slice_width // LANES
    cols = -(-2 * SLOTS * tiles // ROWS)
    rest = tiles - 2 * cols
    assert 0 <= 2 * rest <= cols
    return cols, rest


def dot(a, b):
    return jnp.dot(a, b, preferred_element_type=F32)


def dot_nt(a, b):
    return lax.dot_general(a, b, (((1,), (1,)), ((), ())), preferred_element_type=F32)


def dot_tn(a, b):
    return lax.dot_general(a, b, (((0,), (0,)), ((), ())), preferred_element_type=F32)


def iota(shape, dim):
    return lax.broadcasted_iota(jnp.int32, shape, dim)


def tile_cols(value, start, count):
    return value[:, start * LANES : (start + count) * LANES]


def slot_in_part(i):
    return jnp.where(
        i < 3, i, jnp.where(i < 6, i - 3, jnp.where(i < 9, i - 6, jnp.where(i < 12, i - 9, i - 12)))
    )


def exchange_kernel(
    experts, heads,
    tok_ref, dy_ref, routes_ref, weight_ref, gate_hbm, up_hbm, down_hbm,
    x_ref, d_ref, act_ref, back_ref,
    gate_w, up_w, down_w, turn, send1, recv1, send2, pair_send, pair_recv, y_send, y_recv,
    w_sem, own_sem, s1_sem, r1_sem, s2_sem, r2_sem, ps_sem, pr_sem, ys_sem, yr_sem, as_sem, ar_sem,
):
    total = experts * heads
    cores, y_size = 2, heads // 2
    ctx, head = lax.axis_index("ctx"), lax.axis_index("head")
    me = ctx * heads + head
    core, y = head % cores, head // cores
    toks = tok_ref.shape[0]
    picks = routes_ref.shape[1]
    slice_width, hidden = gate_w.shape
    half = hidden // 2
    cols, rest = block_cols(slice_width)
    part_rows = total * SLOTS
    group_rows = 16 * SLOTS
    sibling = {"ctx": ctx, "head": y * cores + 1 - core}

    weight_copies = [
        pltpu.make_async_copy(src, dst, w_sem.at[n])
        for n, (src, dst) in enumerate(((gate_hbm, gate_w), (up_hbm, up_w), (down_hbm, down_w)))
    ]
    for copy in weight_copies:
        copy.start()

    barrier = pltpu.get_barrier_semaphore()

    def greet(step, carry):
        j = (me + step) % total
        pl.semaphore_signal(
            barrier, inc=1, device_id={"ctx": j // heads, "head": j % heads}, device_id_type=MESH
        )
        return carry

    lax.fori_loop(1, total, greet, 0)

    turn[...] = jnp.zeros_like(turn)
    turn[:, :picks] = routes_ref[...].astype(F32)
    routes_t = turn[...].T[:picks]
    turn[:, :picks] = weight_ref[...]
    weight_t = turn[...].T[:picks]
    out_rows = experts * ROWS
    row = iota((out_rows, 1), 0)
    row_expert = (row // ROWS).astype(F32)
    i = row % ROWS
    hit = jnp.zeros((out_rows, toks), F32)
    pick_weight = jnp.zeros((out_rows, toks), F32)
    for k in range(picks):
        same = routes_t[k : k + 1] == row_expert
        hit = jnp.where(same, 1.0, hit)
        pick_weight = jnp.where(same, weight_t[k : k + 1], pick_weight)
    earlier = (iota((toks, toks), 0) < iota((toks, toks), 1)).astype(BF16)
    position = dot(hit.astype(BF16), earlier)

    def fill(part):
        want = (slot_in_part(i) + part * SLOTS).astype(F32)
        chosen = jnp.where((position == want) & (i < 15), hit, 0.0)
        slot_weight = jnp.sum(chosen * pick_weight, axis=1, keepdims=True)
        picked, scale = [], []
        for kind in range(2):
            second = ((i >= 3) & (i < 6)) | ((i >= 9) & (i < 12))
            if kind:
                second = second | (i >= 12)
            picked.append(
                jnp.concatenate(
                    [jnp.where(second, 0.0, chosen), jnp.where(second, chosen, 0.0)], axis=1
                ).astype(BF16)
            )
            scale.append(jnp.where(second, slot_weight, 1.0))
        for h in range(heads):
            width = pl.ds(h * slice_width, slice_width)
            source = jnp.concatenate([tok_ref[:, width], dy_ref[:, width]], axis=0)
            full = dot(picked[0], source) * scale[0]
            tail = dot(picked[1], tile_cols(source, 2 * cols, rest)) * scale[1]
            for j in range(cols):
                value = jnp.where(i < 6, tile_cols(full, j, 1), tile_cols(full, cols + j, 1))
                if j < 2 * rest:
                    last = tile_cols(tail, j // 2, 1) if j % 2 else tile_cols(full, 2 * cols + j // 2, 1)
                    value = jnp.where(i < 12, value, last)
                send1[part, h, :, :, j * LANES : (j + 1) * LANES] = value.astype(BF16).reshape(
                    experts, ROWS, LANES
                )

    def ship(part):
        pltpu.make_async_copy(
            send1.at[part, head, ctx], recv1.at[part, me], own_sem.at[part]
        ).start()

        def one(step, carry):
            j = (me + step) % total
            e, h = j // heads, j % heads
            pltpu.make_async_remote_copy(
                src_ref=send1.at[part, h, e],
                dst_ref=recv1.at[part, me],
                send_sem=s1_sem.at[part],
                recv_sem=r1_sem.at[part],
                device_id={"ctx": e, "head": h},
                device_id_type=MESH,
            ).start()
            return carry

        lax.fori_loop(1, total, one, 0)

    def wait_blocks(part, sem):
        blocks = recv1.at[part, pl.ds(0, total - 1)]
        pltpu.make_async_copy(blocks, blocks, sem.at[part]).wait()

    fill(0)
    pl.semaphore_wait(barrier, total - 1)
    ship(0)
    for part in range(1, PARTS):
        fill(part)
        ship(part)
    for copy in weight_copies:
        copy.wait()

    def places(first, rows_out):
        out, col = iota((rows_out, 16 * ROWS), 0), iota((rows_out, 16 * ROWS), 1)
        kind = (out >= group_rows).astype(jnp.int32)
        slot = out - kind * group_rows
        return (col == (slot // 3) * ROWS + slot % 3 + kind * 3 + first).astype(BF16)

    place = [places(0, 2 * group_rows), places(6, 2 * group_rows), places(12, group_rows)]

    def activate(part, sums):
        gate, up, back = sums[:, :half], sums[:, half : 2 * half], sums[:, 2 * half :]
        sig = jax.nn.sigmoid(gate)
        smooth = gate * sig
        slope = sig * (1.0 + gate * (1.0 - sig))
        act_ref[part, core, :, :half] = (smooth * up).astype(BF16)
        act_ref[part, core, :, half : 2 * half] = (back * up * slope).astype(BF16)
        act_ref[part, core, :, 2 * half :] = (back * smooth).astype(BF16)

    def project(x, d, side):
        units = pl.ds(pl.multiple_of(side * half, half), half)
        return dot(x, gate_w[:, units]), dot(x, up_w[:, units]), dot_nt(d, down_w[units, :])

    def work(part, carry):
        pltpu.make_async_copy(
            send1.at[part, head, ctx], recv1.at[part, me], own_sem.at[part]
        ).wait()
        wait_blocks(part, r1_sem)
        for g in range(total // 16):
            block = recv1[part, pl.ds(g * 16, 16)].reshape(16 * ROWS, cols * LANES)
            at = pl.ds(pl.multiple_of(part * part_rows + g * group_rows, 16), group_rows)
            for band in range(2):
                value = dot(place[band], block).astype(BF16)
                span = pl.ds(band * cols * LANES, cols * LANES)
                x_ref[at, span] = value[:group_rows]
                d_ref[at, span] = value[group_rows:]
            tail = dot(place[2], tile_cols(block, 0, 2 * rest)).astype(BF16)
            for q in range(rest):
                span = pl.ds((2 * cols + q) * LANES, LANES)
                x_ref[at, span] = tile_cols(tail, 2 * q, 1)
                d_ref[at, span] = tile_cols(tail, 2 * q + 1, 1)

        at = pl.ds(pl.multiple_of(part * part_rows, 16), part_rows)
        x, d = x_ref[at, :], d_ref[at, :]
        for n, value in enumerate(project(x, d, 1 - core)):
            pair_send[part, :, n * half : (n + 1) * half] = value
        to_pair = pltpu.make_async_remote_copy(
            src_ref=pair_send.at[part],
            dst_ref=pair_recv.at[part],
            send_sem=ps_sem.at[part],
            recv_sem=pr_sem.at[part],
            device_id=sibling,
            device_id_type=MESH,
        )
        to_pair.start()
        mine = jnp.concatenate(project(x, d, core), axis=1)
        to_pair.wait_recv()
        mine = mine + pair_recv[part]
        y_send[part] = mine.astype(BF16)
        to_y = []
        for q in range(1, y_size):
            to_y.append(
                pltpu.make_async_remote_copy(
                    src_ref=y_send.at[part],
                    dst_ref=y_recv.at[part, q - 1],
                    send_sem=ys_sem.at[part, q - 1],
                    recv_sem=yr_sem.at[part, q - 1],
                    device_id={"ctx": ctx, "head": ((y + q) % y_size) * cores + core},
                    device_id_type=MESH,
                )
            )
            to_y[-1].start()
        for q, copy in enumerate(to_y):
            copy.wait_recv()
            mine = mine + y_recv[part, q].astype(F32)
        activate(part, mine)
        act_copy = pltpu.make_async_remote_copy(
            src_ref=act_ref.at[part, core],
            dst_ref=act_ref.at[part, core],
            send_sem=as_sem.at[part],
            recv_sem=ar_sem.at[part],
            device_id=sibling,
            device_id_type=MESH,
        )
        act_copy.start()
        act_copy.wait_recv()

        out, grad = 0.0, 0.0
        for side in range(2):
            units = pl.ds(side * half, half)
            out += dot(act_ref[part, side, :, :half], down_w[units, :])
            grad += dot_nt(act_ref[part, side, :, half : 2 * half], gate_w[:, units])
            grad += dot_nt(act_ref[part, side, :, 2 * half :], up_w[:, units])
        out, grad = out.astype(BF16), grad.astype(BF16)
        for g in range(total // 16):
            rows = slice(g * group_rows, (g + 1) * group_rows)
            both = jnp.concatenate([out[rows], grad[rows]], axis=0)
            block = dot_tn(place[0], tile_cols(both, 0, cols)) + dot_tn(
                place[1], tile_cols(both, cols, cols)
            )
            tail = []
            for q in range(rest):
                tail += [tile_cols(v, 2 * cols + q, 1) for v in (out[rows], grad[rows])]
            tail = dot_tn(place[2], jnp.concatenate(tail, axis=1))
            span = 2 * rest * LANES
            block = block.reshape(16, ROWS, cols * LANES)
            send2[part, pl.ds(g * 16, 16), :, :span] = (
                block[:, :, :span] + tail.reshape(16, ROWS, span)
            ).astype(BF16)
            if span < cols * LANES:
                send2[part, pl.ds(g * 16, 16), :, span:] = block[:, :, span:].astype(BF16)

        pltpu.make_async_copy(
            send2.at[part, me], back_ref.at[part, me], own_sem.at[PARTS + part]
        ).start()

        def one(step, inner):
            j = (me + step) % total
            pltpu.make_async_remote_copy(
                src_ref=send2.at[part, j],
                dst_ref=back_ref.at[part, me],
                send_sem=s2_sem.at[part],
                recv_sem=r2_sem.at[part],
                device_id={"ctx": j // heads, "head": j % heads},
                device_id_type=MESH,
            ).start()
            return inner

        lax.fori_loop(1, total, one, 0)
        to_pair.wait_send()
        for copy in to_y:
            copy.wait_send()
        act_copy.wait_send()
        return carry

    lax.fori_loop(0, PARTS, work, 0)

    for part in range(PARTS):
        wait_blocks(part, s1_sem)
        wait_blocks(part, s2_sem)
        pltpu.make_async_copy(
            send2.at[part, me], back_ref.at[part, me], own_sem.at[PARTS + part]
        ).wait()
        wait_blocks(part, r2_sem)


def finish_kernel(
    experts, heads,
    routes_ref, weight_ref, dy_ref, back_ref, x_ref, d_ref, act_ref,
    moe_ref, grad_tok_ref, grad_route_ref, gate_ref, up_ref, down_ref,
    weighted, plain, inner,
):
    step = pl.program_id(0)
    toks, picks = routes_ref.shape
    slice_width = dy_ref.shape[1]
    cols, rest = block_cols(slice_width)
    width = experts * ROWS
    half = act_ref.shape[3] // 3
    lane = iota((1, width), 1)
    lane_expert = lane // ROWS
    i = lane % ROWS

    @pl.when(step == 0)
    def _():
        hit = jnp.zeros((toks, width), F32)
        pick_weight = jnp.zeros((toks, width), F32)
        for k in range(picks):
            same = routes_ref[:, k : k + 1] == lane_expert
            hit = jnp.where(same, 1.0, hit)
            pick_weight = jnp.where(same, weight_ref[:, k : k + 1], pick_weight)
        earlier = (iota((toks, toks), 0) > iota((toks, toks), 1)).astype(BF16)
        position = dot(earlier, hit.astype(BF16))
        for part in range(PARTS):
            want = (slot_in_part(i) + part * SLOTS).astype(F32)
            chosen = jnp.where((position == want) & (i < 15), hit, 0.0)
            scaled = chosen * pick_weight
            high = scaled.astype(BF16)
            low = (scaled - high.astype(F32)).astype(BF16)
            for band in range(3):
                first = (i >= 6 * band) & (i < 6 * band + 3)
                second = first if band == 2 else (i >= 6 * band + 3) & (i < 6 * band + 6)
                zero = jnp.zeros((), BF16)
                weighted[part, band, :, :width] = jnp.where(first, high, zero)
                weighted[part, band, :, width:] = jnp.where(first, low, zero)
                plain[band, :, part * width : (part + 1) * width] = jnp.where(
                    second, chosen, 0.0
                ).astype(BF16)
        inner[...] = jnp.zeros_like(inner)

    blocks = [back_ref[part, :, 0].reshape(width, cols * LANES) for part in range(PARTS)]
    odd = [jnp.concatenate([tile_cols(b, 2 * q + 1, 1) for q in range(rest)], axis=1) for b in blocks]
    even = [jnp.concatenate([tile_cols(b, 2 * q, 1) for q in range(rest)], axis=1) for b in blocks]
    for band, firsts, seconds, start, count in (
        (0, blocks, blocks, 0, cols),
        (1, blocks, blocks, cols, cols),
        (2, even, odd, 2 * cols, rest),
    ):
        span = slice(start * LANES, (start + count) * LANES)
        moe = 0.0
        for part in range(PARTS):
            moe += dot(weighted[part, band], jnp.concatenate([firsts[part]] * 2, axis=0))
            inner[part, band] += dot_nt(dy_ref[:, span], firsts[part])
        moe_ref[:, span] = moe.astype(BF16)
        grad_tok_ref[:, span] = dot(plain[band], jnp.concatenate(seconds, axis=0)).astype(BF16)

    @pl.when(step == pl.num_programs(0) - 1)
    def _():
        found = 0.0
        for part in range(PARTS):
            for band in range(3):
                chosen = weighted[part, band, :, :width].astype(F32) > 0.0
                found += jnp.where(chosen, inner[part, band], 0.0)
        for k in range(picks):
            grad_route_ref[:, k : k + 1] = jnp.sum(
                jnp.where(routes_ref[:, k : k + 1] == lane_expert, found, 0.0), axis=1, keepdims=True
            )

    count = down_ref.shape[0]
    side_steps = half // count
    offset = (step % side_steps) * count

    def units(start):
        at = pl.ds(pl.multiple_of(start * half + offset, count), count)
        return jnp.concatenate(
            [act_ref[part, step // side_steps, :, at] for part in range(PARTS)], axis=0
        )

    gate_ref[...] = dot_tn(x_ref[...], units(1)).astype(BF16)
    up_ref[...] = dot_tn(x_ref[...], units(2)).astype(BF16)
    down_ref[...] = dot_tn(units(0), d_ref[...]).astype(BF16)


def on_device(tokens, routes, route_weight, w_gate, w_up, w_down, grad_out):
    experts = lax.axis_size("ctx")
    heads = lax.axis_size("head")
    total = experts * heads
    toks, model_width = tokens.shape
    picks = routes.shape[1]
    slice_width, hidden = w_gate.shape[1:]
    half = hidden // 2
    cols, rest = block_cols(slice_width)
    part_rows = total * SLOTS
    all_rows = PARTS * part_rows
    y_others = max(1, heads // 2 - 1)
    vmem = pl.BlockSpec(memory_space=pltpu.VMEM)
    hbm = pl.BlockSpec(memory_space=pl.ANY)
    block = (ROWS, cols * LANES)
    dma = pltpu.SemaphoreType.DMA
    x_rows, d_rows, acts, back = pl.pallas_call(
        functools.partial(exchange_kernel, experts, heads),
        out_shape=(
            jax.ShapeDtypeStruct((all_rows, slice_width), BF16),
            jax.ShapeDtypeStruct((all_rows, slice_width), BF16),
            jax.ShapeDtypeStruct((PARTS, 2, part_rows, 3 * half), BF16),
            jax.ShapeDtypeStruct((PARTS, total) + block, BF16),
        ),
        in_specs=[vmem] * 4 + [hbm] * 3,
        out_specs=(vmem,) * 4,
        scratch_shapes=[
            pltpu.VMEM((slice_width, hidden), BF16),
            pltpu.VMEM((slice_width, hidden), BF16),
            pltpu.VMEM((hidden, slice_width), BF16),
            pltpu.VMEM((toks, LANES), F32),
            pltpu.VMEM((PARTS, heads, experts) + block, BF16),
            pltpu.VMEM((PARTS, total) + block, BF16),
            pltpu.VMEM((PARTS, total) + block, BF16),
            pltpu.VMEM((PARTS, part_rows, 3 * half), F32),
            pltpu.VMEM((PARTS, part_rows, 3 * half), F32),
            pltpu.VMEM((PARTS, part_rows, 3 * half), BF16),
            pltpu.VMEM((PARTS, y_others, part_rows, 3 * half), BF16),
            dma((3,)),
            dma((2 * PARTS,)),
            dma((PARTS,)),
            dma((PARTS,)),
            dma((PARTS,)),
            dma((PARTS,)),
            dma((PARTS,)),
            dma((PARTS,)),
            dma((PARTS, y_others)),
            dma((PARTS, y_others)),
            dma((PARTS,)),
            dma((PARTS,)),
        ],
        compiler_params=pltpu.CompilerParams(
            collective_id=0, has_side_effects=True, vmem_limit_bytes=VMEM_BYTES
        ),
    )(tokens, grad_out, routes, route_weight, w_gate[0], w_up[0], w_down[0])

    back = back.reshape((PARTS, experts, heads) + block)

    def whole(shape):
        return pl.BlockSpec(shape, lambda h: (0,) * len(shape))

    units = hidden // heads
    moe_out, grad_tokens, grad_route, grad_gate, grad_up, grad_down = pl.pallas_call(
        functools.partial(finish_kernel, experts, heads),
        grid=(heads,),
        in_specs=[
            whole((toks, picks)),
            whole((toks, picks)),
            pl.BlockSpec((toks, slice_width), lambda h: (0, h)),
            pl.BlockSpec((PARTS, experts, 1) + block, lambda h: (0, 0, h, 0, 0)),
            whole((all_rows, slice_width)),
            whole((all_rows, slice_width)),
            whole((PARTS, 2, part_rows, 3 * half)),
        ],
        out_specs=(
            pl.BlockSpec((toks, slice_width), lambda h: (0, h)),
            pl.BlockSpec((toks, slice_width), lambda h: (0, h)),
            whole((toks, picks)),
            pl.BlockSpec((slice_width, units), lambda h: (0, h)),
            pl.BlockSpec((slice_width, units), lambda h: (0, h)),
            pl.BlockSpec((units, slice_width), lambda h: (h, 0)),
        ),
        out_shape=(
            jax.ShapeDtypeStruct((toks, model_width), BF16),
            jax.ShapeDtypeStruct((toks, model_width), BF16),
            jax.ShapeDtypeStruct((toks, picks), F32),
            jax.ShapeDtypeStruct((slice_width, hidden), BF16),
            jax.ShapeDtypeStruct((slice_width, hidden), BF16),
            jax.ShapeDtypeStruct((hidden, slice_width), BF16),
        ),
        scratch_shapes=[
            pltpu.VMEM((PARTS, 3, toks, 2 * experts * ROWS), BF16),
            pltpu.VMEM((3, toks, PARTS * experts * ROWS), BF16),
            pltpu.VMEM((PARTS, 3, toks, experts * ROWS), F32),
        ],
        compiler_params=pltpu.CompilerParams(vmem_limit_bytes=VMEM_BYTES),
    )(routes, route_weight, grad_out, back, x_rows, d_rows, acts)
    return (moe_out, grad_tokens, grad_route, grad_gate[None], grad_up[None], grad_down[None])


def solution(mesh):
    tok = P(("ctx", "head"), None)
    col, row = P("ctx", "head", None), P("ctx", None, "head")
    return jax.shard_map(
        on_device,
        mesh=mesh,
        in_specs=(tok, tok, tok, col, col, row, tok),
        out_specs=(tok, tok, tok, col, col, row),
        check_vma=False,
    )
```

```python
import functools

import jax
import jax.numpy as jnp
from jax import lax
from jax.experimental import pallas as pl
from jax.experimental.pallas import tpu as pltpu
from jax.sharding import PartitionSpec as P

CAP = 6
PARTS = 2
SLOTS = CAP // PARTS
PIECES = 2
ROWS = 16
LANES = 128
MESH = pl.DeviceIdType.MESH
F32 = jnp.float32
BF16 = jnp.bfloat16
VMEM_BYTES = 60 * 1024 * 1024


def block_cols(slice_width):
    tiles = slice_width // LANES
    cols = -(-2 * SLOTS * tiles // ROWS)
    rest = tiles - 2 * cols
    assert 0 <= 2 * rest <= cols
    return cols, rest


def dot(a, b):
    return jnp.dot(a, b, preferred_element_type=F32)


def dot_nt(a, b):
    return lax.dot_general(a, b, (((1,), (1,)), ((), ())), preferred_element_type=F32)


def dot_tn(a, b):
    return lax.dot_general(a, b, (((0,), (0,)), ((), ())), preferred_element_type=F32)


def iota(shape, dim):
    return lax.broadcasted_iota(jnp.int32, shape, dim)


def tile_cols(value, start, count):
    return value[:, start * LANES : (start + count) * LANES]


def slot_in_part(i):
    return jnp.where(
        i < 3, i, jnp.where(i < 6, i - 3, jnp.where(i < 9, i - 6, jnp.where(i < 12, i - 9, i - 12)))
    )


def exchange_kernel(
    experts, heads,
    tok_hbm, dy_hbm, routes_ref, weight_ref, gate_hbm, up_hbm, down_hbm,
    xt_hbm, d_hbm, act_hbm, hidt_hbm, weighted_hbm, plain_hbm, back_hbm,
    tok_ref, dy_ref, gate_w, up_w, down_w, gate_t, up_t, down_t,
    x_ref, d_ref, act_ref, xt_ref, hidt_ref, weighted, plain,
    send1, recv1, send2, pair_send, pair_recv, y_send, y_recv,
    t_sem, w_sem, o_sem, own_sem, s1_sem, r1_sem, s2_sem, r2_sem,
    ps_sem, pr_sem, ys_sem, yr_sem, as_sem, ar_sem,
):
    total = experts * heads
    cores, y_size = 2, heads // 2
    ctx, head = lax.axis_index("ctx"), lax.axis_index("head")
    me = ctx * heads + head
    core, y = head % cores, head // cores
    toks = tok_ref.shape[0]
    picks = routes_ref.shape[0]
    slice_width, hidden = gate_w.shape
    half = hidden // 2
    piece = half // PIECES
    cols, rest = block_cols(slice_width)
    part_rows = total * SLOTS
    group_rows = 16 * SLOTS
    sibling = {"ctx": ctx, "head": y * cores + 1 - core}

    def local(pairs, sem):
        return [pltpu.make_async_copy(src, dst, sem.at[n]) for n, (src, dst) in enumerate(pairs)]

    token_copies = local(((tok_hbm, tok_ref), (dy_hbm, dy_ref)), t_sem)
    weight_copies = local(((gate_hbm, gate_w), (up_hbm, up_w), (down_hbm, down_w)), w_sem)
    for copy in token_copies:
        copy.start()

    barrier = pltpu.get_barrier_semaphore()

    def greet(step, carry):
        j = (me + step) % total
        pl.semaphore_signal(
            barrier, inc=1, device_id={"ctx": j // heads, "head": j % heads}, device_id_type=MESH
        )
        return carry

    lax.fori_loop(1, total, greet, 0)

    routes_t, weight_t = routes_ref[...], weight_ref[...]
    out_rows = experts * ROWS
    row = iota((out_rows, 1), 0)
    row_expert = row // ROWS
    i = row % ROWS
    hit = jnp.zeros((out_rows, toks), F32)
    pick_weight = jnp.zeros((out_rows, toks), F32)
    for k in range(picks):
        same = routes_t[k : k + 1] == row_expert
        hit = jnp.where(same, 1.0, hit)
        pick_weight = jnp.where(same, weight_t[k : k + 1], pick_weight)
    earlier = (iota((toks, toks), 0) < iota((toks, toks), 1)).astype(BF16)
    position = dot(hit.astype(BF16), earlier)

    def choose(part):
        want = (slot_in_part(i) + part * SLOTS).astype(F32)
        return jnp.where((position == want) & (i < 15), hit, 0.0)

    def fill_and_ship(part):
        chosen = choose(part)
        slot_weight = jnp.sum(chosen * pick_weight, axis=1, keepdims=True)
        picked, scale = [], []
        for kind in range(2):
            second = ((i >= 3) & (i < 6)) | ((i >= 9) & (i < 12))
            if kind:
                second = second | (i >= 12)
            picked.append(
                jnp.concatenate(
                    [jnp.where(second, 0.0, chosen), jnp.where(second, chosen, 0.0)], axis=1
                ).astype(BF16)
            )
            scale.append(jnp.where(second, slot_weight, 1.0))
        for turn in range(heads):
            h = (head + turn) % heads
            width = pl.ds(pl.multiple_of(h * slice_width, LANES), slice_width)
            source = jnp.concatenate([tok_ref[:, width], dy_ref[:, width]], axis=0)
            full = dot(picked[0], source) * scale[0]
            tail = dot(picked[1], tile_cols(source, 2 * cols, rest)) * scale[1]
            for j in range(cols):
                value = jnp.where(i < 6, tile_cols(full, j, 1), tile_cols(full, cols + j, 1))
                if j < 2 * rest:
                    last = tile_cols(tail, j // 2, 1) if j % 2 else tile_cols(full, 2 * cols + j // 2, 1)
                    value = jnp.where(i < 12, value, last)
                send1[part, h, :, :, j * LANES : (j + 1) * LANES] = value.astype(BF16).reshape(
                    experts, ROWS, LANES
                )
            if part == 0 and turn == 0:
                pl.semaphore_wait(barrier, total - 1)

            def one(step, carry):
                e = (ctx + step) % experts
                pltpu.make_async_remote_copy(
                    src_ref=send1.at[part, h, e],
                    dst_ref=recv1.at[part, me],
                    send_sem=s1_sem.at[part],
                    recv_sem=r1_sem.at[part],
                    device_id={"ctx": e, "head": h},
                    device_id_type=MESH,
                ).start()
                return carry

            if turn == 0:
                pltpu.make_async_copy(
                    send1.at[part, head, ctx], recv1.at[part, me], own_sem.at[part]
                ).start()
            lax.fori_loop(0 if turn else 1, experts, one, 0)

    def wait_blocks(part, sem):
        blocks = recv1.at[part, pl.ds(0, total - 1)]
        pltpu.make_async_copy(blocks, blocks, sem.at[part]).wait()

    for copy in token_copies:
        copy.wait()
    for copy in weight_copies:
        copy.start()
    for part in range(PARTS):
        fill_and_ship(part)
    for copy in weight_copies:
        copy.wait()

    def flip(n, carry):
        at = pl.ds(pl.multiple_of(n * LANES, LANES), LANES)
        gate_t[:, at] = gate_w[at, :].T
        up_t[:, at] = up_w[at, :].T
        down_t[at, :] = down_w[:, at].T
        return carry

    lax.fori_loop(0, slice_width // LANES, flip, 0)

    for part in range(PARTS):
        chosen = choose(part)
        scaled = chosen * pick_weight
        high = scaled.astype(BF16).astype(F32)
        low = scaled - high
        for band in range(3):
            first = (i >= 6 * band) & (i < 6 * band + 3)
            second = first if band == 2 else (i >= 6 * band + 3) & (i < 6 * band + 6)
            weighted[part, band, :, :out_rows] = jnp.where(first, high, 0.0).T.astype(BF16)
            weighted[part, band, :, out_rows:] = jnp.where(first, low, 0.0).T.astype(BF16)
            plain[band, :, part * out_rows : (part + 1) * out_rows] = jnp.where(
                second, chosen, 0.0
            ).T.astype(BF16)

    def places(first, rows_out):
        out, col = iota((rows_out, 16 * ROWS), 0), iota((rows_out, 16 * ROWS), 1)
        kind = (out >= group_rows).astype(jnp.int32)
        slot = out - kind * group_rows
        return (col == (slot // 3) * ROWS + slot % 3 + kind * 3 + first).astype(BF16)

    place = [places(0, 2 * group_rows), places(6, 2 * group_rows), places(12, group_rows)]

    def activate(part, p, sums):
        gate, up, back = (sums[:, n * piece : (n + 1) * piece] for n in range(3))
        sig = jax.nn.sigmoid(gate)
        smooth = gate * sig
        slope = sig * (1.0 + gate * (1.0 - sig))
        act_ref[part, core, p, :, :piece] = (smooth * up).astype(BF16)
        act_ref[part, core, p, :, piece : 2 * piece] = (back * up * slope).astype(BF16)
        act_ref[part, core, p, :, 2 * piece :] = (back * smooth).astype(BF16)

    def units_of(side, p):
        return pl.ds(pl.multiple_of(side * half + p * piece, piece), piece)

    def project(x, d, side, p):
        units = units_of(side, p)
        return dot(x, gate_w[:, units]), dot(x, up_w[:, units]), dot(d, down_t[:, units])

    def work(part, carry):
        pltpu.make_async_copy(
            send1.at[part, head, ctx], recv1.at[part, me], own_sem.at[part]
        ).wait()
        wait_blocks(part, r1_sem)
        for g in range(total // 16):
            block = recv1[part, pl.ds(g * 16, 16)].reshape(16 * ROWS, cols * LANES)
            at = pl.ds(pl.multiple_of(part * part_rows + g * group_rows, 16), group_rows)
            for band in range(2):
                value = dot(place[band], block).astype(BF16)
                span = pl.ds(band * cols * LANES, cols * LANES)
                x_ref[at, span] = value[:group_rows]
                d_ref[at, span] = value[group_rows:]
            tail = dot(place[2], tile_cols(block, 0, 2 * rest)).astype(BF16)
            for q in range(rest):
                span = pl.ds((2 * cols + q) * LANES, LANES)
                x_ref[at, span] = tile_cols(tail, 2 * q, 1)
                d_ref[at, span] = tile_cols(tail, 2 * q + 1, 1)

        at = pl.ds(pl.multiple_of(part * part_rows, 16), part_rows)
        x, d = x_ref[at, :], d_ref[at, :]
        to_pair, to_y, to_act = [], [], []
        for p in range(PIECES):
            for n, value in enumerate(project(x, d, 1 - core, p)):
                pair_send[part, p, :, n * piece : (n + 1) * piece] = value
            to_pair.append(
                pltpu.make_async_remote_copy(
                    src_ref=pair_send.at[part, p],
                    dst_ref=pair_recv.at[part, p],
                    send_sem=ps_sem.at[part, p],
                    recv_sem=pr_sem.at[part, p],
                    device_id=sibling,
                    device_id_type=MESH,
                )
            )
            to_pair[-1].start()
        sums = []
        for p in range(PIECES):
            mine = jnp.concatenate(project(x, d, core, p), axis=1)
            to_pair[p].wait_recv()
            mine = mine + pair_recv[part, p]
            sums.append(mine)
            y_send[part, p] = mine.astype(BF16)
            to_y.append([])
            for q in range(1, y_size):
                to_y[-1].append(
                    pltpu.make_async_remote_copy(
                        src_ref=y_send.at[part, p],
                        dst_ref=y_recv.at[part, p, q - 1],
                        send_sem=ys_sem.at[part, p, q - 1],
                        recv_sem=yr_sem.at[part, p, q - 1],
                        device_id={"ctx": ctx, "head": ((y + q) % y_size) * cores + core},
                        device_id_type=MESH,
                    )
                )
                to_y[-1][-1].start()
        for p in range(PIECES):
            mine = sums[p]
            for q, copy in enumerate(to_y[p]):
                copy.wait_recv()
                mine = mine + y_recv[part, p, q].astype(F32)
            activate(part, p, mine)
            to_act.append(
                pltpu.make_async_remote_copy(
                    src_ref=act_ref.at[part, core, p],
                    dst_ref=act_ref.at[part, core, p],
                    send_sem=as_sem.at[part, p],
                    recv_sem=ar_sem.at[part, p],
                    device_id=sibling,
                    device_id_type=MESH,
                )
            )
            to_act[-1].start()

        out, grad = 0.0, 0.0
        for far in range(2):
            side = 1 - core if far else core
            for p in range(PIECES):
                if far:
                    to_act[p].wait_recv()
                units = units_of(side, p)
                out += dot(act_ref[part, side, p, :, :piece], down_w[units, :])
                grad += dot(act_ref[part, side, p, :, piece : 2 * piece], gate_t[units, :])
                grad += dot(act_ref[part, side, p, :, 2 * piece :], up_t[units, :])
        out, grad = out.astype(BF16), grad.astype(BF16)
        for g in range(total // 16):
            rows = slice(g * group_rows, (g + 1) * group_rows)
            both = jnp.concatenate([out[rows], grad[rows]], axis=0)
            block = dot_tn(place[0], tile_cols(both, 0, cols)) + dot_tn(
                place[1], tile_cols(both, cols, cols)
            )
            tail = []
            for q in range(rest):
                tail += [tile_cols(v, 2 * cols + q, 1) for v in (out[rows], grad[rows])]
            tail = dot_tn(place[2], jnp.concatenate(tail, axis=1))
            span = 2 * rest * LANES
            block = block.reshape(16, ROWS, cols * LANES)
            send2[part, pl.ds(g * 16, 16), :, :span] = (
                block[:, :, :span] + tail.reshape(16, ROWS, span)
            ).astype(BF16)
            if span < cols * LANES:
                send2[part, pl.ds(g * 16, 16), :, span:] = block[:, :, span:].astype(BF16)

        pltpu.make_async_copy(
            send2.at[part, me], back_hbm.at[part, me], own_sem.at[PARTS + part]
        ).start()

        def one(step, inner):
            j = (me + step) % total
            pltpu.make_async_remote_copy(
                src_ref=send2.at[part, j],
                dst_ref=back_hbm.at[part, me],
                send_sem=s2_sem.at[part],
                recv_sem=r2_sem.at[part],
                device_id={"ctx": j // heads, "head": j % heads},
                device_id_type=MESH,
            ).start()
            return inner

        lax.fori_loop(1, total, one, 0)
        for p in range(PIECES):
            to_pair[p].wait_send()
            for copy in to_y[p]:
                copy.wait_send()
            to_act[p].wait_send()
        return carry

    lax.fori_loop(0, PARTS, work, 0)

    xt_ref[...] = x_ref[...].T
    for side in range(2):
        for p in range(PIECES):
            start = side * half + p * piece
            hidt_ref[start : start + piece, :] = jnp.concatenate(
                [act_ref[part, side, p, :, :piece] for part in range(PARTS)], axis=0
            ).T
    out_copies = local(
        (
            (xt_ref, xt_hbm), (d_ref, d_hbm), (act_ref, act_hbm), (hidt_ref, hidt_hbm),
            (weighted, weighted_hbm), (plain, plain_hbm),
        ),
        o_sem,
    )
    for copy in out_copies:
        copy.start()
    for part in range(PARTS):
        wait_blocks(part, s1_sem)
        wait_blocks(part, s2_sem)
        pltpu.make_async_copy(
            send2.at[part, me], back_hbm.at[part, me], own_sem.at[PARTS + part]
        ).wait()
    for copy in out_copies:
        copy.wait()
    for part in range(PARTS):
        wait_blocks(part, r2_sem)


def finish_kernel(
    experts,
    routes_ref, dy_ref, back_ref, xt_ref, d_ref, act_ref, hidt_ref, weighted, plain,
    moe_ref, grad_tok_ref, grad_route_ref, gate_ref, up_ref, down_ref,
    inner,
):
    step = pl.program_id(0)
    picks = routes_ref.shape[0]
    slice_width = dy_ref.shape[1]
    cols, rest = block_cols(slice_width)
    width = experts * ROWS

    @pl.when(step == 0)
    def _():
        inner[...] = jnp.zeros_like(inner)

    count = down_ref.shape[0]
    piece = act_ref.shape[4] // 3
    piece_steps = piece // count
    slab, offset = step // piece_steps, (step % piece_steps) * count

    def units(start):
        at = pl.ds(pl.multiple_of(start * piece + offset, count), count)
        return jnp.concatenate(
            [act_ref[part, slab // PIECES, slab % PIECES, :, at] for part in range(PARTS)], axis=0
        )

    gate_ref[...] = dot(xt_ref[...], units(1)).astype(BF16)
    up_ref[...] = dot(xt_ref[...], units(2)).astype(BF16)
    down_ref[...] = dot(hidt_ref[...], d_ref[...]).astype(BF16)

    blocks = [back_ref[part, :, 0].reshape(width, cols * LANES) for part in range(PARTS)]
    odd = [jnp.concatenate([tile_cols(b, 2 * q + 1, 1) for q in range(rest)], axis=1) for b in blocks]
    even = [jnp.concatenate([tile_cols(b, 2 * q, 1) for q in range(rest)], axis=1) for b in blocks]
    for band, firsts, seconds, start, count in (
        (0, blocks, blocks, 0, cols),
        (1, blocks, blocks, cols, cols),
        (2, even, odd, 2 * cols, rest),
    ):
        span = slice(start * LANES, (start + count) * LANES)
        moe = 0.0
        for part in range(PARTS):
            moe += dot(weighted[part, band], jnp.concatenate([firsts[part]] * 2, axis=0))
            inner[part, band] += dot_nt(dy_ref[:, span], firsts[part])
        moe_ref[:, span] = moe.astype(BF16)
        grad_tok_ref[:, span] = dot(plain[band], jnp.concatenate(seconds, axis=0)).astype(BF16)

    @pl.when(step == pl.num_programs(0) - 1)
    def _():
        found = 0.0
        for part in range(PARTS):
            for band in range(3):
                chosen = weighted[part, band, :, :width].astype(F32) > 0.0
                found += jnp.where(chosen, inner[part, band], 0.0)
        found = found.T
        row_expert = iota((width, 1), 0) // ROWS
        for k in range(picks):
            grad_route_ref[k : k + 1, :] = jnp.sum(
                jnp.where(routes_ref[k : k + 1, :] == row_expert, found, 0.0), axis=0, keepdims=True
            )


def on_device(tokens, routes, route_weight, w_gate, w_up, w_down, grad_out):
    experts = lax.axis_size("ctx")
    heads = lax.axis_size("head")
    total = experts * heads
    toks, model_width = tokens.shape
    picks = routes.shape[1]
    slice_width, hidden = w_gate.shape[1:]
    half = hidden // 2
    cols, rest = block_cols(slice_width)
    part_rows = total * SLOTS
    all_rows = PARTS * part_rows
    y_others = max(1, heads // 2 - 1)
    piece = half // PIECES
    slots = experts * ROWS
    vmem = pl.BlockSpec(memory_space=pltpu.VMEM)
    hbm = pl.BlockSpec(memory_space=pl.ANY)
    block = (ROWS, cols * LANES)
    dma = pltpu.SemaphoreType.DMA
    handed = (
        (slice_width, all_rows),
        (all_rows, slice_width),
        (PARTS, 2, PIECES, part_rows, 3 * piece),
        (hidden, all_rows),
        (PARTS, 3, toks, 2 * slots),
        (3, toks, PARTS * slots),
    )
    xt, d_rows, acts, hidt, weighted, plain, back = pl.pallas_call(
        functools.partial(exchange_kernel, experts, heads),
        out_shape=tuple(
            jax.ShapeDtypeStruct(shape, BF16) for shape in handed + ((PARTS, total) + block,)
        ),
        in_specs=[hbm] * 2 + [vmem] * 2 + [hbm] * 3,
        out_specs=(hbm,) * 7,
        scratch_shapes=[
            pltpu.VMEM((toks, model_width), BF16),
            pltpu.VMEM((toks, model_width), BF16),
            pltpu.VMEM((slice_width, hidden), BF16),
            pltpu.VMEM((slice_width, hidden), BF16),
            pltpu.VMEM((hidden, slice_width), BF16),
            pltpu.VMEM((hidden, slice_width), BF16),
            pltpu.VMEM((hidden, slice_width), BF16),
            pltpu.VMEM((slice_width, hidden), BF16),
            pltpu.VMEM(handed[1], BF16),
            pltpu.VMEM(handed[1], BF16),
            pltpu.VMEM(handed[2], BF16),
            pltpu.VMEM(handed[0], BF16),
            pltpu.VMEM(handed[3], BF16),
            pltpu.VMEM(handed[4], BF16),
            pltpu.VMEM(handed[5], BF16),
            pltpu.VMEM((PARTS, heads, experts) + block, BF16),
            pltpu.VMEM((PARTS, total) + block, BF16),
            pltpu.VMEM((PARTS, total) + block, BF16),
            pltpu.VMEM((PARTS, PIECES, part_rows, 3 * piece), F32),
            pltpu.VMEM((PARTS, PIECES, part_rows, 3 * piece), F32),
            pltpu.VMEM((PARTS, PIECES, part_rows, 3 * piece), BF16),
            pltpu.VMEM((PARTS, PIECES, y_others, part_rows, 3 * piece), BF16),
            dma((2,)),
            dma((3,)),
            dma((6,)),
            dma((2 * PARTS,)),
            dma((PARTS,)),
            dma((PARTS,)),
            dma((PARTS,)),
            dma((PARTS,)),
            dma((PARTS, PIECES)),
            dma((PARTS, PIECES)),
            dma((PARTS, PIECES, y_others)),
            dma((PARTS, PIECES, y_others)),
            dma((PARTS, PIECES)),
            dma((PARTS, PIECES)),
        ],
        compiler_params=pltpu.CompilerParams(
            collective_id=0, has_side_effects=True, vmem_limit_bytes=VMEM_BYTES
        ),
    )(tokens, grad_out, routes.T, route_weight.T, w_gate[0], w_up[0], w_down[0])

    back = back.reshape((PARTS, experts, heads) + block)

    def whole(shape):
        return pl.BlockSpec(shape, lambda h: (0,) * len(shape))

    units = hidden // heads
    moe_out, grad_tokens, grad_route, grad_gate, grad_up, grad_down = pl.pallas_call(
        functools.partial(finish_kernel, experts),
        grid=(heads,),
        in_specs=[
            whole((picks, toks)),
            pl.BlockSpec((toks, slice_width), lambda h: (0, h)),
            pl.BlockSpec((PARTS, experts, 1) + block, lambda h: (0, 0, h, 0, 0)),
            whole(handed[0]),
            whole(handed[1]),
            whole(handed[2]),
            pl.BlockSpec((units, all_rows), lambda h: (h, 0)),
            whole(handed[4]),
            whole(handed[5]),
        ],
        out_specs=(
            pl.BlockSpec((toks, slice_width), lambda h: (0, h)),
            pl.BlockSpec((toks, slice_width), lambda h: (0, h)),
            whole((picks, toks)),
            pl.BlockSpec((slice_width, units), lambda h: (0, h)),
            pl.BlockSpec((slice_width, units), lambda h: (0, h)),
            pl.BlockSpec((units, slice_width), lambda h: (h, 0)),
        ),
        out_shape=(
            jax.ShapeDtypeStruct((toks, model_width), BF16),
            jax.ShapeDtypeStruct((toks, model_width), BF16),
            jax.ShapeDtypeStruct((picks, toks), F32),
            jax.ShapeDtypeStruct((slice_width, hidden), BF16),
            jax.ShapeDtypeStruct((slice_width, hidden), BF16),
            jax.ShapeDtypeStruct((hidden, slice_width), BF16),
        ),
        scratch_shapes=[pltpu.VMEM((PARTS, 3, toks, slots), F32)],
        compiler_params=pltpu.CompilerParams(vmem_limit_bytes=VMEM_BYTES),
    )(routes.T, grad_out, back, xt, d_rows, acts, hidt, weighted, plain)
    return (moe_out, grad_tokens, grad_route.T, grad_gate[None], grad_up[None], grad_down[None])


def solution(mesh):
    tok = P(("ctx", "head"), None)
    col, row = P("ctx", "head", None), P("ctx", None, "head")
    return jax.shard_map(
        on_device,
        mesh=mesh,
        in_specs=(tok, tok, tok, col, col, row, tok),
        out_specs=(tok, tok, tok, col, col, row),
        check_vma=False,
    )
```

```python
import functools

import jax
import jax.numpy as jnp
from jax import lax
from jax.experimental import pallas as pl
from jax.experimental.pallas import tpu as pltpu
from jax.sharding import PartitionSpec as P

CAP = 6
SPLIT = (4, 2)
PARTS = len(SPLIT)
PIECES = 2
ROWS = 16
LANES = 128
MESH = pl.DeviceIdType.MESH
F32 = jnp.float32
BF16 = jnp.bfloat16
VMEM_BYTES = 60 * 1024 * 1024


class Form:
    def __init__(self, part, slice_width):
        self.slots = SPLIT[part]
        self.first = sum(SPLIT[:part])
        self.height = 2 * self.slots
        self.bands = ROWS // self.height
        tiles = slice_width // LANES
        self.cols = -(-tiles // self.bands)
        self.block = (ROWS, self.cols * LANES)
        self.spans = [
            (b * self.cols, min(self.cols, tiles - b * self.cols)) for b in range(self.bands)
        ]


def forms(slice_width):
    return [Form(part, slice_width) for part in range(PARTS)]


def dot(a, b):
    return jnp.dot(a, b, preferred_element_type=F32)


def dot_nt(a, b):
    return lax.dot_general(a, b, (((1,), (1,)), ((), ())), preferred_element_type=F32)


def iota(shape, dim):
    return lax.broadcasted_iota(jnp.int32, shape, dim)


def tile_cols(value, start, count):
    return value[:, start * LANES : (start + count) * LANES]


def exchange_kernel(
    experts, heads,
    tok_hbm, dy_hbm, routes_ref, weight_ref, gate_hbm, up_hbm, down_hbm,
    xt_hbm, d_hbm, act_hbm, hidt_hbm, select_hbm, back0_hbm, back1_hbm,
    tok_ref, dy_ref, gate_w, up_w, down_w, gate_t, up_t, down_t,
    x_ref, d_ref, act_ref, xt_ref, hidt_ref, select,
    out0, out1, in0, in1, ret0, ret1, pair_send, pair_recv, y_send, y_recv,
    t_sem, w_sem, o_sem, own_sem, s1_sem, r1_sem, s2_sem, r2_sem,
    ps_sem, pr_sem, ys_sem, yr_sem, as_sem, ar_sem,
):
    total = experts * heads
    cores, y_size = 2, heads // 2
    ctx, head = lax.axis_index("ctx"), lax.axis_index("head")
    me = ctx * heads + head
    core, y = head % cores, head // cores
    toks = tok_ref.shape[0]
    picks = routes_ref.shape[0]
    slice_width, hidden = gate_w.shape
    half = hidden // 2
    piece = half // PIECES
    form = forms(slice_width)
    send1, recv1, send2, back = (out0, out1), (in0, in1), (ret0, ret1), (back0_hbm, back1_hbm)
    sibling = {"ctx": ctx, "head": y * cores + 1 - core}

    def local(pairs, sem):
        return [pltpu.make_async_copy(src, dst, sem.at[n]) for n, (src, dst) in enumerate(pairs)]

    token_copies = local(((tok_hbm, tok_ref), (dy_hbm, dy_ref)), t_sem)
    weight_copies = local(((gate_hbm, gate_w), (up_hbm, up_w), (down_hbm, down_w)), w_sem)
    for copy in token_copies:
        copy.start()

    barrier = pltpu.get_barrier_semaphore()

    def greet(step, carry):
        j = (me + step) % total
        pl.semaphore_signal(
            barrier, inc=1, device_id={"ctx": j // heads, "head": j % heads}, device_id_type=MESH
        )
        return carry

    lax.fori_loop(1, total, greet, 0)

    routes_t, weight_t = routes_ref[...], weight_ref[...]
    out_rows = experts * ROWS
    row = iota((out_rows, 1), 0)
    row_expert = row // ROWS
    i = row % ROWS
    hit = jnp.zeros((out_rows, toks), F32)
    pick_weight = jnp.zeros((out_rows, toks), F32)
    for k in range(picks):
        same = routes_t[k : k + 1] == row_expert
        hit = jnp.where(same, 1.0, hit)
        pick_weight = jnp.where(same, weight_t[k : k + 1], pick_weight)
    earlier = (iota((toks, toks), 0) < iota((toks, toks), 1)).astype(BF16)
    position = dot(hit.astype(BF16), earlier)

    def choose(f):
        want = (i % f.slots + f.first).astype(F32)
        return jnp.where(position == want, hit, 0.0), i % f.height >= f.slots

    def own_in(part):
        return pltpu.make_async_copy(
            send1[part].at[head, ctx], recv1[part].at[me], own_sem.at[part]
        )

    def own_back(part):
        return pltpu.make_async_copy(
            send2[part].at[ctx, head], back[part].at[me], own_sem.at[PARTS + part]
        )

    def send_turn(part, turn, returning):
        h = (head + turn) % heads

        def one(step, carry):
            e = (ctx + step) % experts
            pltpu.make_async_remote_copy(
                src_ref=send2[part].at[e, h] if returning else send1[part].at[h, e],
                dst_ref=back[part].at[me] if returning else recv1[part].at[me],
                send_sem=(s2_sem if returning else s1_sem).at[part],
                recv_sem=(r2_sem if returning else r1_sem).at[part],
                device_id={"ctx": e, "head": h},
                device_id_type=MESH,
            ).start()
            return carry

        if turn == 0:
            (own_back if returning else own_in)(part).start()
        lax.fori_loop(0 if turn else 1, experts, one, 0)

    def send_quarters(part, quarters, returning):
        for q in quarters:
            for turn in range(q * heads // 4, (q + 1) * heads // 4):
                send_turn(part, turn, returning)

    def fill(part, picked, scale, turn):
        f = form[part]
        h = (head + turn) % heads
        width = pl.ds(pl.multiple_of(h * slice_width, LANES), slice_width)
        source = jnp.concatenate([tok_ref[:, width], dy_ref[:, width]], axis=0)
        full = dot(picked, source) * scale
        for j in range(f.cols):
            value = tile_cols(full, j, 1)
            for b in range(1, f.bands):
                if j < f.spans[b][1]:
                    value = jnp.where(
                        i < b * f.height, value, tile_cols(full, b * f.cols + j, 1)
                    )
            send1[part][h, :, :, j * LANES : (j + 1) * LANES] = value.astype(BF16).reshape(
                experts, ROWS, LANES
            )

    def wait_blocks(part, sem):
        blocks = recv1[part].at[pl.ds(0, total - 1)]
        pltpu.make_async_copy(blocks, blocks, sem.at[part]).wait()

    for copy in token_copies:
        copy.wait()
    for copy in weight_copies:
        copy.start()
    for part in range(PARTS):
        chosen, second = choose(form[part])
        slot_weight = jnp.sum(chosen * pick_weight, axis=1, keepdims=True)
        picked = jnp.concatenate(
            [jnp.where(second, 0.0, chosen), jnp.where(second, chosen, 0.0)], axis=1
        ).astype(BF16)
        scale = jnp.where(second, slot_weight, 1.0)
        for turn in range(heads):
            fill(part, picked, scale, turn)
            if part == 0:
                if turn == 0:
                    pl.semaphore_wait(barrier, total - 1)
                send_turn(part, turn, False)
    send_quarters(1, (0, 1), False)
    for copy in weight_copies:
        copy.wait()

    def flip(n, carry):
        at = pl.ds(pl.multiple_of(n * LANES, LANES), LANES)
        gate_t[:, at] = gate_w[at, :].T
        up_t[:, at] = up_w[at, :].T
        down_t[at, :] = down_w[:, at].T
        return carry

    lax.fori_loop(0, slice_width // LANES, flip, 0)

    n = 0
    for part in range(PARTS):
        f = form[part]
        chosen, second = choose(f)
        scaled = chosen * pick_weight
        high = scaled.astype(BF16).astype(F32)
        low = scaled - high
        for b in range(f.bands):
            band = i // f.height == b
            first = band & ~second
            select[n, :toks, :out_rows] = jnp.where(first, high, 0.0).T.astype(BF16)
            select[n, :toks, out_rows:] = jnp.where(first, low, 0.0).T.astype(BF16)
            select[n, toks:, :out_rows] = jnp.where(band & second, chosen, 0.0).T.astype(BF16)
            select[n, toks:, out_rows:] = jnp.zeros((toks, out_rows), BF16)
            n += 1

    def place(f, b, turned):
        count = 2 * 16 * f.slots
        shape = (16 * ROWS, count) if turned else (count, 16 * ROWS)
        out, src = iota(shape, int(turned)), iota(shape, 1 - int(turned))
        kind = (out >= count // 2).astype(jnp.int32)
        slot = out - kind * (count // 2)
        from_row = (slot // f.slots) * ROWS + slot % f.slots + kind * f.slots + b * f.height
        return (src == from_row).astype(BF16)

    def activate(rows, p, sums):
        gate, up, back_grad = (sums[:, n * piece : (n + 1) * piece] for n in range(3))
        sig = jax.nn.sigmoid(gate)
        smooth = gate * sig
        slope = sig * (1.0 + gate * (1.0 - sig))
        act_ref[core, p, rows, :piece] = (smooth * up).astype(BF16)
        act_ref[core, p, rows, piece : 2 * piece] = (back_grad * up * slope).astype(BF16)
        act_ref[core, p, rows, 2 * piece :] = (back_grad * smooth).astype(BF16)

    def units_of(side, p):
        return pl.ds(pl.multiple_of(side * half + p * piece, piece), piece)

    def project(x, d, side, p):
        units = units_of(side, p)
        return dot(x, gate_w[:, units]), dot(x, up_w[:, units]), dot(d, down_t[:, units])

    def work(part, beside_sums, beside_acts):
        f = form[part]
        rows = pl.ds(f.first * total, f.slots * total)
        group_rows = 16 * f.slots
        own_in(part).wait()
        wait_blocks(part, r1_sem)
        places = [place(f, b, False) for b in range(f.bands)]
        for g in range(total // 16):
            block = recv1[part][pl.ds(g * 16, 16)].reshape(16 * ROWS, f.cols * LANES)
            at = pl.ds(f.first * total + g * group_rows, group_rows)
            for b, (start, count) in enumerate(f.spans):
                value = dot(places[b], tile_cols(block, 0, count)).astype(BF16)
                span = pl.ds(start * LANES, count * LANES)
                x_ref[at, span] = value[:group_rows]
                d_ref[at, span] = value[group_rows:]

        x, d = x_ref[rows, :], d_ref[rows, :]
        to_pair, to_y, to_act = [], [], []
        for p in range(PIECES):
            for n, value in enumerate(project(x, d, 1 - core, p)):
                pair_send[p, rows, n * piece : (n + 1) * piece] = value
            to_pair.append(
                pltpu.make_async_remote_copy(
                    src_ref=pair_send.at[p, rows],
                    dst_ref=pair_recv.at[p, rows],
                    send_sem=ps_sem.at[part, p],
                    recv_sem=pr_sem.at[part, p],
                    device_id=sibling,
                    device_id_type=MESH,
                )
            )
            to_pair[-1].start()
        sums = []
        for p in range(PIECES):
            mine = jnp.concatenate(project(x, d, core, p), axis=1)
            to_pair[p].wait_recv()
            mine = mine + pair_recv[p, rows]
            sums.append(mine)
            y_send[p, rows] = mine.astype(BF16)
            to_y.append([])
            for q in range(1, y_size):
                to_y[-1].append(
                    pltpu.make_async_remote_copy(
                        src_ref=y_send.at[p, rows],
                        dst_ref=y_recv.at[q - 1, p, rows],
                        send_sem=ys_sem.at[part, p, q - 1],
                        recv_sem=yr_sem.at[part, p, q - 1],
                        device_id={"ctx": ctx, "head": ((y + q) % y_size) * cores + core},
                        device_id_type=MESH,
                    )
                )
                to_y[-1][-1].start()
        beside_sums()
        for p in range(PIECES):
            mine = sums[p]
            for q, copy in enumerate(to_y[p]):
                copy.wait_recv()
                mine = mine + y_recv[q, p, rows].astype(F32)
            activate(rows, p, mine)
            to_act.append(
                pltpu.make_async_remote_copy(
                    src_ref=act_ref.at[core, p, rows],
                    dst_ref=act_ref.at[core, p, rows],
                    send_sem=as_sem.at[part, p],
                    recv_sem=ar_sem.at[part, p],
                    device_id=sibling,
                    device_id_type=MESH,
                )
            )
            to_act[-1].start()
        beside_acts()

        out, grad = 0.0, 0.0
        for far in range(2):
            side = 1 - core if far else core
            for p in range(PIECES):
                if far:
                    to_act[p].wait_recv()
                units = units_of(side, p)
                out += dot(act_ref[side, p, rows, :piece], down_w[units, :])
                grad += dot(act_ref[side, p, rows, piece : 2 * piece], gate_t[units, :])
                grad += dot(act_ref[side, p, rows, 2 * piece :], up_t[units, :])
        out, grad = out.astype(BF16), grad.astype(BF16)
        places = [place(f, b, True) for b in range(f.bands)]
        for g in range(total // 16):
            at = slice(g * group_rows, (g + 1) * group_rows)
            both = jnp.concatenate([out[at], grad[at]], axis=0)
            block = 0.0
            for b, (start, count) in enumerate(f.spans):
                band = dot(places[b], tile_cols(both, start, count))
                if count < f.cols:
                    gap = jnp.zeros((16 * ROWS, (f.cols - count) * LANES), F32)
                    band = jnp.concatenate([band, gap], axis=1)
                block += band
            send2[part][pl.ds(g * 16 // heads, 16 // heads)] = block.astype(BF16).reshape(
                (16 // heads, heads) + f.block
            )
        return to_pair + sum(to_y, []) + to_act

    started = work(
        0, lambda: send_quarters(1, (2,), False), lambda: send_quarters(1, (3,), False)
    )
    send_quarters(0, (0,), True)
    started += work(
        1, lambda: send_quarters(0, (1,), True), lambda: send_quarters(0, (2, 3), True)
    )
    send_quarters(1, range(4), True)

    xt_ref[...] = x_ref[...].T
    for side in range(2):
        for p in range(PIECES):
            start = side * half + p * piece
            hidt_ref[start : start + piece, :] = act_ref[side, p, :, :piece].T
    out_copies = local(
        (
            (xt_ref, xt_hbm), (d_ref, d_hbm), (act_ref, act_hbm), (hidt_ref, hidt_hbm),
            (select, select_hbm),
        ),
        o_sem,
    )
    for copy in out_copies:
        copy.start()
    for copy in started:
        copy.wait_send()
    for part in range(PARTS):
        wait_blocks(part, s1_sem)
        wait_blocks(part, s2_sem)
        own_back(part).wait()
    for copy in out_copies:
        copy.wait()
    for part in range(PARTS):
        wait_blocks(part, r2_sem)


def finish_kernel(
    experts,
    routes_ref, dy_ref, back0_ref, back1_ref, xt_ref, d_ref, act_ref, hidt_ref, select,
    moe_ref, grad_tok_ref, grad_route_ref, gate_ref, up_ref, down_ref,
    inner,
):
    step = pl.program_id(0)
    picks, toks = routes_ref.shape
    slice_width = dy_ref.shape[1]
    width = experts * ROWS

    @pl.when(step == 0)
    def _():
        inner[...] = jnp.zeros_like(inner)

    count = down_ref.shape[0]
    piece = act_ref.shape[3] // 3
    piece_steps = piece // count
    slab, offset = step // piece_steps, (step % piece_steps) * count

    def units(start):
        at = pl.ds(pl.multiple_of(start * piece + offset, count), count)
        return act_ref[slab // PIECES, slab % PIECES, :, at]

    gate_ref[...] = dot(xt_ref[...], units(1)).astype(BF16)
    up_ref[...] = dot(xt_ref[...], units(2)).astype(BF16)
    down_ref[...] = dot(hidt_ref[...], d_ref[...]).astype(BF16)

    combined, n = 0.0, 0
    for f, back_ref in zip(forms(slice_width), (back0_ref, back1_ref)):
        block = back_ref[:, 0].reshape(width, f.cols * LANES)
        twice = jnp.concatenate([block, block], axis=0)
        bands = []
        for start, count in f.spans:
            bands.append(dot(select[n], tile_cols(twice, 0, count)))
            span = slice(start * LANES, (start + count) * LANES)
            inner[n] += dot_nt(dy_ref[:, span], tile_cols(block, 0, count))
            n += 1
        combined += jnp.concatenate(bands, axis=1)
    moe_ref[...] = combined[:toks].astype(BF16)
    grad_tok_ref[...] = combined[toks:].astype(BF16)

    @pl.when(step == pl.num_programs(0) - 1)
    def _():
        found = 0.0
        for n in range(inner.shape[0]):
            chosen = select[n, :toks, :width].astype(F32) > 0.0
            found += jnp.where(chosen, inner[n], 0.0)
        found = found.T
        row_expert = iota((width, 1), 0) // ROWS
        for k in range(picks):
            grad_route_ref[k : k + 1, :] = jnp.sum(
                jnp.where(routes_ref[k : k + 1, :] == row_expert, found, 0.0), axis=0, keepdims=True
            )


def on_device(tokens, routes, route_weight, w_gate, w_up, w_down, grad_out):
    experts = lax.axis_size("ctx")
    heads = lax.axis_size("head")
    total = experts * heads
    toks, model_width = tokens.shape
    picks = routes.shape[1]
    slice_width, hidden = w_gate.shape[1:]
    all_rows = CAP * total
    y_others = max(1, heads // 2 - 1)
    piece = hidden // 2 // PIECES
    slots = experts * ROWS
    form = forms(slice_width)
    bands = sum(f.bands for f in form)
    vmem = pl.BlockSpec(memory_space=pltpu.VMEM)
    hbm = pl.BlockSpec(memory_space=pl.ANY)
    dma = pltpu.SemaphoreType.DMA
    handed = (
        (slice_width, all_rows),
        (all_rows, slice_width),
        (2, PIECES, all_rows, 3 * piece),
        (hidden, all_rows),
        (bands, 2 * toks, 2 * slots),
    )
    sums = (PIECES, all_rows, 3 * piece)
    xt, d_rows, acts, hidt, select, *back = pl.pallas_call(
        functools.partial(exchange_kernel, experts, heads),
        out_shape=tuple(
            jax.ShapeDtypeStruct(shape, BF16)
            for shape in handed + tuple((total,) + f.block for f in form)
        ),
        in_specs=[hbm] * 2 + [vmem] * 2 + [hbm] * 3,
        out_specs=(hbm,) * 7,
        scratch_shapes=[
            pltpu.VMEM((toks, model_width), BF16),
            pltpu.VMEM((toks, model_width), BF16),
            pltpu.VMEM((slice_width, hidden), BF16),
            pltpu.VMEM((slice_width, hidden), BF16),
            pltpu.VMEM((hidden, slice_width), BF16),
            pltpu.VMEM((hidden, slice_width), BF16),
            pltpu.VMEM((hidden, slice_width), BF16),
            pltpu.VMEM((slice_width, hidden), BF16),
            pltpu.VMEM(handed[1], BF16),
            pltpu.VMEM(handed[1], BF16),
            pltpu.VMEM(handed[2], BF16),
            pltpu.VMEM(handed[0], BF16),
            pltpu.VMEM(handed[3], BF16),
            pltpu.VMEM(handed[4], BF16),
            *(pltpu.VMEM((heads, experts) + f.block, BF16) for f in form),
            *(pltpu.VMEM((total,) + f.block, BF16) for f in form),
            *(pltpu.VMEM((experts, heads) + f.block, BF16) for f in form),
            pltpu.VMEM(sums, F32),
            pltpu.VMEM(sums, F32),
            pltpu.VMEM(sums, BF16),
            pltpu.VMEM((y_others,) + sums, BF16),
            dma((2,)),
            dma((3,)),
            dma((5,)),
            dma((2 * PARTS,)),
            dma((PARTS,)),
            dma((PARTS,)),
            dma((PARTS,)),
            dma((PARTS,)),
            dma((PARTS, PIECES)),
            dma((PARTS, PIECES)),
            dma((PARTS, PIECES, y_others)),
            dma((PARTS, PIECES, y_others)),
            dma((PARTS, PIECES)),
            dma((PARTS, PIECES)),
        ],
        compiler_params=pltpu.CompilerParams(
            collective_id=0, has_side_effects=True, vmem_limit_bytes=VMEM_BYTES
        ),
    )(tokens, grad_out, routes.T, route_weight.T, w_gate[0], w_up[0], w_down[0])

    back = [b.reshape((experts, heads) + f.block) for b, f in zip(back, form)]

    def whole(shape):
        return pl.BlockSpec(shape, lambda h: (0,) * len(shape))

    units = hidden // heads
    moe_out, grad_tokens, grad_route, grad_gate, grad_up, grad_down = pl.pallas_call(
        functools.partial(finish_kernel, experts),
        grid=(heads,),
        in_specs=[
            whole((picks, toks)),
            pl.BlockSpec((toks, slice_width), lambda h: (0, h)),
            *(pl.BlockSpec((experts, 1) + f.block, lambda h: (0, h, 0, 0)) for f in form),
            whole(handed[0]),
            whole(handed[1]),
            whole(handed[2]),
            pl.BlockSpec((units, all_rows), lambda h: (h, 0)),
            whole(handed[4]),
        ],
        out_specs=(
            pl.BlockSpec((toks, slice_width), lambda h: (0, h)),
            pl.BlockSpec((toks, slice_width), lambda h: (0, h)),
            whole((picks, toks)),
            pl.BlockSpec((slice_width, units), lambda h: (0, h)),
            pl.BlockSpec((slice_width, units), lambda h: (0, h)),
            pl.BlockSpec((units, slice_width), lambda h: (h, 0)),
        ),
        out_shape=(
            jax.ShapeDtypeStruct((toks, model_width), BF16),
            jax.ShapeDtypeStruct((toks, model_width), BF16),
            jax.ShapeDtypeStruct((picks, toks), F32),
            jax.ShapeDtypeStruct((slice_width, hidden), BF16),
            jax.ShapeDtypeStruct((slice_width, hidden), BF16),
            jax.ShapeDtypeStruct((hidden, slice_width), BF16),
        ),
        scratch_shapes=[pltpu.VMEM((bands, toks, slots), F32)],
        compiler_params=pltpu.CompilerParams(vmem_limit_bytes=VMEM_BYTES),
    )(routes.T, grad_out, *back, xt, d_rows, acts, hidt, select)
    return (moe_out, grad_tokens, grad_route.T, grad_gate[None], grad_up[None], grad_down[None])


def solution(mesh):
    tok = P(("ctx", "head"), None)
    col, row = P("ctx", "head", None), P("ctx", None, "head")
    return jax.shard_map(
        on_device,
        mesh=mesh,
        in_specs=(tok, tok, tok, col, col, row, tok),
        out_specs=(tok, tok, tok, col, col, row),
        check_vma=False,
    )
```

```python
import functools

import jax
import jax.numpy as jnp
from jax import lax
from jax.experimental import pallas as pl
from jax.experimental.pallas import tpu as pltpu
from jax.sharding import PartitionSpec as P

CAP = 6
SPLIT = (4, 2)
PARTS = len(SPLIT)
PIECES = 1
ROWS = 16
LANES = 128
MESH = pl.DeviceIdType.MESH
F32 = jnp.float32
BF16 = jnp.bfloat16
VMEM_BYTES = 60 * 1024 * 1024


class Form:
    def __init__(self, part, slice_width):
        self.slots = SPLIT[part]
        self.first = sum(SPLIT[:part])
        self.height = 2 * self.slots
        self.bands = ROWS // self.height
        tiles = slice_width // LANES
        self.cols = -(-tiles // self.bands)
        self.block = (ROWS, self.cols * LANES)
        self.spans = [
            (b * self.cols, min(self.cols, tiles - b * self.cols)) for b in range(self.bands)
        ]


def forms(slice_width):
    return [Form(part, slice_width) for part in range(PARTS)]


def dot(a, b):
    return jnp.dot(a, b, preferred_element_type=F32)


def dot_nt(a, b):
    return lax.dot_general(a, b, (((1,), (1,)), ((), ())), preferred_element_type=F32)


def iota(shape, dim):
    return lax.broadcasted_iota(jnp.int32, shape, dim)


def tile_cols(value, start, count):
    return value[:, start * LANES : (start + count) * LANES]


def exchange_kernel(
    experts, heads,
    tok_hbm, dy_hbm, routes_ref, weight_ref, gate_hbm, up_hbm, down_hbm,
    xt_hbm, d_hbm, act_hbm, hidt_hbm, select_hbm, back0_hbm, back1_hbm,
    tok_ref, dy_ref, pair_w, down_w, pair_t, down_t,
    x_ref, d_ref, act_ref, xt_ref, hidt_ref, select,
    out0, out1, in0, in1, ret0, ret1, pair_send, pair_recv, y_send, y_recv,
    t_sem, w_sem, o_sem, own_sem, s1_sem, r1_sem, s2_sem, r2_sem,
    ps_sem, pr_sem, ys_sem, yr_sem, as_sem, ar_sem,
):
    total = experts * heads
    cores, y_size = 2, heads // 2
    ctx, head = lax.axis_index("ctx"), lax.axis_index("head")
    me = ctx * heads + head
    core, y = head % cores, head // cores
    toks = tok_ref.shape[0]
    picks = routes_ref.shape[0]
    hidden, slice_width = down_w.shape
    half = hidden // 2
    piece = half // PIECES
    form = forms(slice_width)
    send1, recv1, send2, back = (out0, out1), (in0, in1), (ret0, ret1), (back0_hbm, back1_hbm)
    sibling = {"ctx": ctx, "head": y * cores + 1 - core}

    def local(pairs, sem):
        return [pltpu.make_async_copy(src, dst, sem.at[n]) for n, (src, dst) in enumerate(pairs)]

    token_copies = local(((tok_hbm, tok_ref), (dy_hbm, dy_ref)), t_sem)
    weight_moves = [(down_hbm, down_w)]
    for slab in range(2 * PIECES):
        for n, src in enumerate((gate_hbm, up_hbm)):
            weight_moves.append(
                (
                    src.at[:, pl.ds(slab * piece, piece)],
                    pair_w.at[slab, :, pl.ds(n * piece, piece)],
                )
            )
    weight_copies = local(weight_moves, w_sem)
    for copy in token_copies:
        copy.start()

    barrier = pltpu.get_barrier_semaphore()

    def greet(step, carry):
        j = (me + step) % total
        pl.semaphore_signal(
            barrier, inc=1, device_id={"ctx": j // heads, "head": j % heads}, device_id_type=MESH
        )
        return carry

    lax.fori_loop(1, total, greet, 0)

    routes_t, weight_t = routes_ref[...], weight_ref[...]
    out_rows = experts * ROWS
    row = iota((out_rows, 1), 0)
    row_expert = row // ROWS
    i = row % ROWS
    hit = jnp.zeros((out_rows, toks), F32)
    pick_weight = jnp.zeros((out_rows, toks), F32)
    for k in range(picks):
        same = routes_t[k : k + 1] == row_expert
        hit = jnp.where(same, 1.0, hit)
        pick_weight = jnp.where(same, weight_t[k : k + 1], pick_weight)
    earlier = (iota((toks, toks), 0) < iota((toks, toks), 1)).astype(BF16)
    position = dot(hit.astype(BF16), earlier)

    def choose(f):
        want = (i % f.slots + f.first).astype(F32)
        return jnp.where(position == want, hit, 0.0), i % f.height >= f.slots

    def own_in(part):
        return pltpu.make_async_copy(
            send1[part].at[head, ctx], recv1[part].at[me], own_sem.at[part]
        )

    def own_back(part):
        return pltpu.make_async_copy(
            send2[part].at[ctx, head], back[part].at[me], own_sem.at[PARTS + part]
        )

    def send_turn(part, turn, returning):
        h = (head + turn) % heads

        def one(step, carry):
            e = (ctx + step) % experts
            pltpu.make_async_remote_copy(
                src_ref=send2[part].at[e, h] if returning else send1[part].at[h, e],
                dst_ref=back[part].at[me] if returning else recv1[part].at[me],
                send_sem=(s2_sem if returning else s1_sem).at[part],
                recv_sem=(r2_sem if returning else r1_sem).at[part],
                device_id={"ctx": e, "head": h},
                device_id_type=MESH,
            ).start()
            return carry

        if turn == 0:
            (own_back if returning else own_in)(part).start()
        lax.fori_loop(0 if turn else 1, experts, one, 0)

    def send_all(part, returning):
        for turn in range(heads):
            send_turn(part, turn, returning)

    def fill(part, picked, scale, turn):
        f = form[part]
        h = (head + turn) % heads
        width = pl.ds(pl.multiple_of(h * slice_width, LANES), slice_width)
        source = jnp.concatenate([tok_ref[:, width], dy_ref[:, width]], axis=0)
        full = dot(picked, source) * scale
        for j in range(f.cols):
            value = tile_cols(full, j, 1)
            for b in range(1, f.bands):
                if j < f.spans[b][1]:
                    value = jnp.where(
                        i < b * f.height, value, tile_cols(full, b * f.cols + j, 1)
                    )
            send1[part][h, :, :, j * LANES : (j + 1) * LANES] = value.astype(BF16).reshape(
                experts, ROWS, LANES
            )

    def wait_blocks(part, sem):
        blocks = recv1[part].at[pl.ds(0, total - 1)]
        pltpu.make_async_copy(blocks, blocks, sem.at[part]).wait()

    for copy in token_copies:
        copy.wait()
    for copy in weight_copies:
        copy.start()
    for part in range(PARTS):
        chosen, second = choose(form[part])
        slot_weight = jnp.sum(chosen * pick_weight, axis=1, keepdims=True)
        picked = jnp.concatenate(
            [jnp.where(second, 0.0, chosen), jnp.where(second, chosen, 0.0)], axis=1
        ).astype(BF16)
        scale = jnp.where(second, slot_weight, 1.0)
        for turn in range(heads):
            fill(part, picked, scale, turn)
            if part == 0 and turn == 0:
                pl.semaphore_wait(barrier, total - 1)
            send_turn(part, turn, False)
    for copy in weight_copies:
        copy.wait()

    def flip(n, carry):
        at = pl.ds(pl.multiple_of(n * LANES, LANES), LANES)
        for slab in range(2 * PIECES):
            pair_t[slab, :, at] = pair_w[slab, at, :].T
        down_t[at, :] = down_w[:, at].T
        return carry

    lax.fori_loop(0, slice_width // LANES, flip, 0)

    n = 0
    for part in range(PARTS):
        f = form[part]
        chosen, second = choose(f)
        scaled = chosen * pick_weight
        high = scaled.astype(BF16).astype(F32)
        low = scaled - high
        for b in range(f.bands):
            band = i // f.height == b
            first = band & ~second
            select[n, :toks, :out_rows] = jnp.where(first, high, 0.0).T.astype(BF16)
            select[n, :toks, out_rows:] = jnp.where(first, low, 0.0).T.astype(BF16)
            select[n, toks:, :out_rows] = jnp.where(band & second, chosen, 0.0).T.astype(BF16)
            select[n, toks:, out_rows:] = jnp.zeros((toks, out_rows), BF16)
            n += 1

    def place(f, b, turned):
        count = 2 * 16 * f.slots
        shape = (16 * ROWS, count) if turned else (count, 16 * ROWS)
        out, src = iota(shape, int(turned)), iota(shape, 1 - int(turned))
        kind = (out >= count // 2).astype(jnp.int32)
        slot = out - kind * (count // 2)
        from_row = (slot // f.slots) * ROWS + slot % f.slots + kind * f.slots + b * f.height
        return (src == from_row).astype(BF16)

    def activate(rows, p, sums):
        gate, up, back_grad = (sums[:, n * piece : (n + 1) * piece] for n in range(3))
        sig = jax.nn.sigmoid(gate)
        smooth = gate * sig
        slope = sig * (1.0 + gate * (1.0 - sig))
        act_ref[core, p, rows, :piece] = (smooth * up).astype(BF16)
        act_ref[core, p, rows, piece : 2 * piece] = (back_grad * up * slope).astype(BF16)
        act_ref[core, p, rows, 2 * piece :] = (back_grad * smooth).astype(BF16)

    def units_of(side, p):
        return pl.ds(pl.multiple_of(side * half + p * piece, piece), piece)

    def project(x, d, side, p):
        return dot(x, pair_w[side * PIECES + p]), dot(d, down_t[:, units_of(side, p)])

    def work(part):
        f = form[part]
        rows = pl.ds(f.first * total, f.slots * total)
        group_rows = 16 * f.slots
        own_in(part).wait()
        wait_blocks(part, r1_sem)
        places = [place(f, b, False) for b in range(f.bands)]
        for g in range(total // 16):
            block = recv1[part][pl.ds(g * 16, 16)].reshape(16 * ROWS, f.cols * LANES)
            at = pl.ds(f.first * total + g * group_rows, group_rows)
            for b, (start, count) in enumerate(f.spans):
                value = dot(places[b], tile_cols(block, 0, count)).astype(BF16)
                span = pl.ds(start * LANES, count * LANES)
                x_ref[at, span] = value[:group_rows]
                d_ref[at, span] = value[group_rows:]

        x, d = x_ref[rows, :], d_ref[rows, :]
        to_pair, to_y, to_act = [], [], []
        for p in range(PIECES):
            ahead, behind = project(x, d, 1 - core, p)
            pair_send[p, rows, : 2 * piece] = ahead
            pair_send[p, rows, 2 * piece :] = behind
            to_pair.append(
                pltpu.make_async_remote_copy(
                    src_ref=pair_send.at[p, rows],
                    dst_ref=pair_recv.at[p, rows],
                    send_sem=ps_sem.at[part, p],
                    recv_sem=pr_sem.at[part, p],
                    device_id=sibling,
                    device_id_type=MESH,
                )
            )
            to_pair[-1].start()
        sums = []
        for p in range(PIECES):
            mine = jnp.concatenate(project(x, d, core, p), axis=1)
            to_pair[p].wait_recv()
            mine = mine + pair_recv[p, rows]
            sums.append(mine)
            y_send[p, rows] = mine.astype(BF16)
            to_y.append([])
            for q in range(1, y_size):
                to_y[-1].append(
                    pltpu.make_async_remote_copy(
                        src_ref=y_send.at[p, rows],
                        dst_ref=y_recv.at[q - 1, p, rows],
                        send_sem=ys_sem.at[part, p, q - 1],
                        recv_sem=yr_sem.at[part, p, q - 1],
                        device_id={"ctx": ctx, "head": ((y + q) % y_size) * cores + core},
                        device_id_type=MESH,
                    )
                )
                to_y[-1][-1].start()
        for p in range(PIECES):
            mine = sums[p]
            for q, copy in enumerate(to_y[p]):
                copy.wait_recv()
                mine = mine + y_recv[q, p, rows].astype(F32)
            activate(rows, p, mine)
            to_act.append(
                pltpu.make_async_remote_copy(
                    src_ref=act_ref.at[core, p, rows],
                    dst_ref=act_ref.at[core, p, rows],
                    send_sem=as_sem.at[part, p],
                    recv_sem=ar_sem.at[part, p],
                    device_id=sibling,
                    device_id_type=MESH,
                )
            )
            to_act[-1].start()

        out, grad = 0.0, 0.0
        for far in range(2):
            side = 1 - core if far else core
            for p in range(PIECES):
                if far:
                    to_act[p].wait_recv()
                units = units_of(side, p)
                out += dot(act_ref[side, p, rows, :piece], down_w[units, :])
                grad += dot(act_ref[side, p, rows, piece:], pair_t[side * PIECES + p])
        out, grad = out.astype(BF16), grad.astype(BF16)
        places = [place(f, b, True) for b in range(f.bands)]
        for g in range(total // 16):
            at = slice(g * group_rows, (g + 1) * group_rows)
            both = jnp.concatenate([out[at], grad[at]], axis=0)
            block = 0.0
            for b, (start, count) in enumerate(f.spans):
                band = dot(places[b], tile_cols(both, start, count))
                if count < f.cols:
                    gap = jnp.zeros((16 * ROWS, (f.cols - count) * LANES), F32)
                    band = jnp.concatenate([band, gap], axis=1)
                block += band
            send2[part][pl.ds(g * 16 // heads, 16 // heads)] = block.astype(BF16).reshape(
                (16 // heads, heads) + f.block
            )
        return to_pair + sum(to_y, []) + to_act

    started = work(0)
    send_all(0, True)
    started += work(1)
    send_all(1, True)

    xt_ref[...] = x_ref[...].T
    for side in range(2):
        for p in range(PIECES):
            start = side * half + p * piece
            hidt_ref[start : start + piece, :] = act_ref[side, p, :, :piece].T
    out_copies = local(
        (
            (xt_ref, xt_hbm), (d_ref, d_hbm), (act_ref, act_hbm), (hidt_ref, hidt_hbm),
            (select, select_hbm),
        ),
        o_sem,
    )
    for copy in out_copies:
        copy.start()
    for copy in started:
        copy.wait_send()
    for part in range(PARTS):
        wait_blocks(part, s1_sem)
        wait_blocks(part, s2_sem)
        own_back(part).wait()
    for copy in out_copies:
        copy.wait()
    for part in range(PARTS):
        wait_blocks(part, r2_sem)


def finish_kernel(
    experts,
    routes_ref, dy_ref, back0_ref, back1_ref, xt_ref, d_ref, act_ref, hidt_ref, select,
    moe_ref, grad_tok_ref, grad_route_ref, gate_ref, up_ref, down_ref,
    inner,
):
    step = pl.program_id(0)
    picks, toks = routes_ref.shape
    slice_width = dy_ref.shape[1]
    width = experts * ROWS

    @pl.when(step == 0)
    def _():
        inner[...] = jnp.zeros_like(inner)

    count = down_ref.shape[0]
    piece = act_ref.shape[3] // 3
    piece_steps = piece // count
    slab, offset = step // piece_steps, (step % piece_steps) * count

    def units(start):
        at = pl.ds(pl.multiple_of(start * piece + offset, count), count)
        return act_ref[slab // PIECES, slab % PIECES, :, at]

    pair = dot(xt_ref[...], jnp.concatenate([units(1), units(2)], axis=1)).astype(BF16)
    gate_ref[...] = pair[:, :count]
    up_ref[...] = pair[:, count:]
    down_ref[...] = dot(hidt_ref[...], d_ref[...]).astype(BF16)

    combined, n = 0.0, 0
    for f, back_ref in zip(forms(slice_width), (back0_ref, back1_ref)):
        block = back_ref[:, 0].reshape(width, f.cols * LANES)
        twice = jnp.concatenate([block, block], axis=0)
        bands = []
        for start, count in f.spans:
            bands.append(dot(select[n], tile_cols(twice, 0, count)))
            span = slice(start * LANES, (start + count) * LANES)
            inner[n] += dot_nt(dy_ref[:, span], tile_cols(block, 0, count))
            n += 1
        combined += jnp.concatenate(bands, axis=1)
    moe_ref[...] = combined[:toks].astype(BF16)
    grad_tok_ref[...] = combined[toks:].astype(BF16)

    @pl.when(step == pl.num_programs(0) - 1)
    def _():
        found = 0.0
        for n in range(inner.shape[0]):
            chosen = select[n, :toks, :width].astype(F32) > 0.0
            found += jnp.where(chosen, inner[n], 0.0)
        found = found.T
        row_expert = iota((width, 1), 0) // ROWS
        for k in range(picks):
            grad_route_ref[k : k + 1, :] = jnp.sum(
                jnp.where(routes_ref[k : k + 1, :] == row_expert, found, 0.0), axis=0, keepdims=True
            )


def on_device(tokens, routes, route_weight, w_gate, w_up, w_down, grad_out):
    experts = lax.axis_size("ctx")
    heads = lax.axis_size("head")
    total = experts * heads
    toks, model_width = tokens.shape
    picks = routes.shape[1]
    slice_width, hidden = w_gate.shape[1:]
    all_rows = CAP * total
    y_others = max(1, heads // 2 - 1)
    piece = hidden // 2 // PIECES
    slots = experts * ROWS
    form = forms(slice_width)
    bands = sum(f.bands for f in form)
    vmem = pl.BlockSpec(memory_space=pltpu.VMEM)
    hbm = pl.BlockSpec(memory_space=pl.ANY)
    dma = pltpu.SemaphoreType.DMA
    handed = (
        (slice_width, all_rows),
        (all_rows, slice_width),
        (2, PIECES, all_rows, 3 * piece),
        (hidden, all_rows),
        (bands, 2 * toks, 2 * slots),
    )
    sums = (PIECES, all_rows, 3 * piece)
    xt, d_rows, acts, hidt, select, *back = pl.pallas_call(
        functools.partial(exchange_kernel, experts, heads),
        out_shape=tuple(
            jax.ShapeDtypeStruct(shape, BF16)
            for shape in handed + tuple((total,) + f.block for f in form)
        ),
        in_specs=[hbm] * 2 + [vmem] * 2 + [hbm] * 3,
        out_specs=(hbm,) * 7,
        scratch_shapes=[
            pltpu.VMEM((toks, model_width), BF16),
            pltpu.VMEM((toks, model_width), BF16),
            pltpu.VMEM((2 * PIECES, slice_width, 2 * piece), BF16),
            pltpu.VMEM((hidden, slice_width), BF16),
            pltpu.VMEM((2 * PIECES, 2 * piece, slice_width), BF16),
            pltpu.VMEM((slice_width, hidden), BF16),
            pltpu.VMEM(handed[1], BF16),
            pltpu.VMEM(handed[1], BF16),
            pltpu.VMEM(handed[2], BF16),
            pltpu.VMEM(handed[0], BF16),
            pltpu.VMEM(handed[3], BF16),
            pltpu.VMEM(handed[4], BF16),
            *(pltpu.VMEM((heads, experts) + f.block, BF16) for f in form),
            *(pltpu.VMEM((total,) + f.block, BF16) for f in form),
            *(pltpu.VMEM((experts, heads) + f.block, BF16) for f in form),
            pltpu.VMEM(sums, F32),
            pltpu.VMEM(sums, F32),
            pltpu.VMEM(sums, BF16),
            pltpu.VMEM((y_others,) + sums, BF16),
            dma((2,)),
            dma((1 + 4 * PIECES,)),
            dma((5,)),
            dma((2 * PARTS,)),
            dma((PARTS,)),
            dma((PARTS,)),
            dma((PARTS,)),
            dma((PARTS,)),
            dma((PARTS, PIECES)),
            dma((PARTS, PIECES)),
            dma((PARTS, PIECES, y_others)),
            dma((PARTS, PIECES, y_others)),
            dma((PARTS, PIECES)),
            dma((PARTS, PIECES)),
        ],
        compiler_params=pltpu.CompilerParams(
            collective_id=0, has_side_effects=True, vmem_limit_bytes=VMEM_BYTES
        ),
    )(tokens, grad_out, routes.T, route_weight.T, w_gate[0], w_up[0], w_down[0])

    back = [b.reshape((experts, heads) + f.block) for b, f in zip(back, form)]

    def whole(shape):
        return pl.BlockSpec(shape, lambda h: (0,) * len(shape))

    units = hidden // heads
    moe_out, grad_tokens, grad_route, grad_gate, grad_up, grad_down = pl.pallas_call(
        functools.partial(finish_kernel, experts),
        grid=(heads,),
        in_specs=[
            whole((picks, toks)),
            pl.BlockSpec((toks, slice_width), lambda h: (0, h)),
            *(pl.BlockSpec((experts, 1) + f.block, lambda h: (0, h, 0, 0)) for f in form),
            whole(handed[0]),
            whole(handed[1]),
            whole(handed[2]),
            pl.BlockSpec((units, all_rows), lambda h: (h, 0)),
            whole(handed[4]),
        ],
        out_specs=(
            pl.BlockSpec((toks, slice_width), lambda h: (0, h)),
            pl.BlockSpec((toks, slice_width), lambda h: (0, h)),
            whole((picks, toks)),
            pl.BlockSpec((slice_width, units), lambda h: (0, h)),
            pl.BlockSpec((slice_width, units), lambda h: (0, h)),
            pl.BlockSpec((units, slice_width), lambda h: (h, 0)),
        ),
        out_shape=(
            jax.ShapeDtypeStruct((toks, model_width), BF16),
            jax.ShapeDtypeStruct((toks, model_width), BF16),
            jax.ShapeDtypeStruct((picks, toks), F32),
            jax.ShapeDtypeStruct((slice_width, hidden), BF16),
            jax.ShapeDtypeStruct((slice_width, hidden), BF16),
            jax.ShapeDtypeStruct((hidden, slice_width), BF16),
        ),
        scratch_shapes=[pltpu.VMEM((bands, toks, slots), F32)],
        compiler_params=pltpu.CompilerParams(vmem_limit_bytes=VMEM_BYTES),
    )(routes.T, grad_out, *back, xt, d_rows, acts, hidt, select)
    return (moe_out, grad_tokens, grad_route.T, grad_gate[None], grad_up[None], grad_down[None])


def solution(mesh):
    tok = P(("ctx", "head"), None)
    col, row = P("ctx", "head", None), P("ctx", None, "head")
    return jax.shard_map(
        on_device,
        mesh=mesh,
        in_specs=(tok, tok, tok, col, col, row, tok),
        out_specs=(tok, tok, tok, col, col, row),
        check_vma=False,
    )
```

```python
import functools

import jax
import jax.numpy as jnp
from jax import lax
from jax.experimental import pallas as pl
from jax.experimental.pallas import tpu as pltpu
from jax.sharding import PartitionSpec as P

CAP = 6
SPLIT = (4, 2)
PARTS = len(SPLIT)
PIECES = 2
ROWS = 16
LANES = 128
MESH = pl.DeviceIdType.MESH
F32 = jnp.float32
BF16 = jnp.bfloat16
VMEM_BYTES = 60 * 1024 * 1024


class Form:
    def __init__(self, part, slice_width):
        self.slots = SPLIT[part]
        self.first = sum(SPLIT[:part])
        self.height = 2 * self.slots
        self.bands = ROWS // self.height
        tiles = slice_width // LANES
        self.cols = -(-tiles // self.bands)
        self.block = (ROWS, self.cols * LANES)
        self.spans = [
            (b * self.cols, min(self.cols, tiles - b * self.cols)) for b in range(self.bands)
        ]


def forms(slice_width):
    return [Form(part, slice_width) for part in range(PARTS)]


def dot(a, b):
    return jnp.dot(a, b, preferred_element_type=F32)


def dot_nt(a, b):
    return lax.dot_general(a, b, (((1,), (1,)), ((), ())), preferred_element_type=F32)


def iota(shape, dim):
    return lax.broadcasted_iota(jnp.int32, shape, dim)


def tile_cols(value, start, count):
    return value[:, start * LANES : (start + count) * LANES]


def exchange_kernel(
    experts, heads,
    tok_hbm, dy_hbm, routes_ref, weight_ref, gate_hbm, up_hbm, down_hbm,
    xt_hbm, d_hbm, act_hbm, hidt_hbm, select_hbm, back0_hbm, back1_hbm,
    tok_ref, dy_ref, pair_w, down_w, pair_t, down_t,
    x_ref, d_ref, act_ref, xt_ref, hidt_ref, select,
    out0, out1, in0, in1, ret0, ret1, pair_send, pair_recv, y_send, y_recv,
    t_sem, w_sem, o_sem, own_sem, s1_sem, r1_sem, s2_sem, r2_sem,
    ps_sem, pr_sem, ys_sem, yr_sem, as_sem, ar_sem,
):
    total = experts * heads
    cores, y_size = 2, heads // 2
    ctx, head = lax.axis_index("ctx"), lax.axis_index("head")
    me = ctx * heads + head
    core, y = head % cores, head // cores
    toks = tok_ref.shape[0]
    picks = routes_ref.shape[0]
    hidden, slice_width = down_w.shape
    half = hidden // 2
    piece = half // PIECES
    form = forms(slice_width)
    send1, recv1, send2, back = (out0, out1), (in0, in1), (ret0, ret1), (back0_hbm, back1_hbm)
    sibling = {"ctx": ctx, "head": y * cores + 1 - core}

    def local(pairs, sem):
        return [pltpu.make_async_copy(src, dst, sem.at[n]) for n, (src, dst) in enumerate(pairs)]

    token_copies = local(((tok_hbm, tok_ref), (dy_hbm, dy_ref)), t_sem)
    weight_moves = [(down_hbm, down_w)]
    for slab in range(2 * PIECES):
        for n, src in enumerate((gate_hbm, up_hbm)):
            weight_moves.append(
                (
                    src.at[:, pl.ds(slab * piece, piece)],
                    pair_w.at[slab, :, pl.ds(n * piece, piece)],
                )
            )
    weight_copies = local(weight_moves, w_sem)
    for copy in token_copies:
        copy.start()

    barrier = pltpu.get_barrier_semaphore()

    def greet(step, carry):
        j = (me + step) % total
        pl.semaphore_signal(
            barrier, inc=1, device_id={"ctx": j // heads, "head": j % heads}, device_id_type=MESH
        )
        return carry

    lax.fori_loop(1, total, greet, 0)

    routes_t, weight_t = routes_ref[...], weight_ref[...]
    out_rows = experts * ROWS
    row = iota((out_rows, 1), 0)
    row_expert = row // ROWS
    i = row % ROWS
    hit = jnp.zeros((out_rows, toks), F32)
    pick_weight = jnp.zeros((out_rows, toks), F32)
    for k in range(picks):
        same = routes_t[k : k + 1] == row_expert
        hit = jnp.where(same, 1.0, hit)
        pick_weight = jnp.where(same, weight_t[k : k + 1], pick_weight)
    earlier = (iota((toks, toks), 0) < iota((toks, toks), 1)).astype(BF16)
    position = dot(hit.astype(BF16), earlier)

    def choose(f):
        want = (i % f.slots + f.first).astype(F32)
        return jnp.where(position == want, hit, 0.0), i % f.height >= f.slots

    def own_in(part):
        return pltpu.make_async_copy(
            send1[part].at[head, ctx], recv1[part].at[me], own_sem.at[part]
        )

    def own_back(part):
        return pltpu.make_async_copy(
            send2[part].at[ctx, head], back[part].at[me], own_sem.at[PARTS + part]
        )

    def send_turn(part, turn, returning):
        h = (head + turn) % heads

        def one(step, carry):
            e = (ctx + step) % experts
            pltpu.make_async_remote_copy(
                src_ref=send2[part].at[e, h] if returning else send1[part].at[h, e],
                dst_ref=back[part].at[me] if returning else recv1[part].at[me],
                send_sem=(s2_sem if returning else s1_sem).at[part],
                recv_sem=(r2_sem if returning else r1_sem).at[part],
                device_id={"ctx": e, "head": h},
                device_id_type=MESH,
            ).start()
            return carry

        if turn == 0:
            (own_back if returning else own_in)(part).start()
        lax.fori_loop(0 if turn else 1, experts, one, 0)

    def send_quarters(part, returning, quarters):
        for q in quarters:
            for turn in range(q * heads // 4, (q + 1) * heads // 4):
                send_turn(part, turn, returning)

    def fill(part, picked, scale, turn):
        f = form[part]
        h = (head + turn) % heads
        width = pl.ds(pl.multiple_of(h * slice_width, LANES), slice_width)
        source = jnp.concatenate([tok_ref[:, width], dy_ref[:, width]], axis=0)
        full = dot(picked, source) * scale
        for j in range(f.cols):
            value = tile_cols(full, j, 1)
            for b in range(1, f.bands):
                if j < f.spans[b][1]:
                    value = jnp.where(
                        i < b * f.height, value, tile_cols(full, b * f.cols + j, 1)
                    )
            send1[part][h, :, :, j * LANES : (j + 1) * LANES] = value.astype(BF16).reshape(
                experts, ROWS, LANES
            )

    def wait_blocks(part, sem):
        blocks = recv1[part].at[pl.ds(0, total - 1)]
        pltpu.make_async_copy(blocks, blocks, sem.at[part]).wait()

    for copy in token_copies:
        copy.wait()
    for copy in weight_copies:
        copy.start()
    for part in range(PARTS):
        chosen, second = choose(form[part])
        slot_weight = jnp.sum(chosen * pick_weight, axis=1, keepdims=True)
        picked = jnp.concatenate(
            [jnp.where(second, 0.0, chosen), jnp.where(second, chosen, 0.0)], axis=1
        ).astype(BF16)
        scale = jnp.where(second, slot_weight, 1.0)
        for turn in range(heads):
            fill(part, picked, scale, turn)
            if part == 0 and turn == 0:
                pl.semaphore_wait(barrier, total - 1)
            if part == 0:
                send_turn(part, turn, False)
    send_quarters(1, False, (0, 1, 2))
    for copy in weight_copies:
        copy.wait()

    def flip(n, carry):
        at = pl.ds(pl.multiple_of(n * LANES, LANES), LANES)
        for slab in range(2 * PIECES):
            pair_t[slab, :, at] = pair_w[slab, at, :].T
        down_t[at, :] = down_w[:, at].T
        return carry

    lax.fori_loop(0, slice_width // LANES, flip, 0)

    n = 0
    for part in range(PARTS):
        f = form[part]
        chosen, second = choose(f)
        scaled = chosen * pick_weight
        high = scaled.astype(BF16).astype(F32)
        low = scaled - high
        for b in range(f.bands):
            band = i // f.height == b
            first = band & ~second
            select[n, :toks, :out_rows] = jnp.where(first, high, 0.0).T.astype(BF16)
            select[n, :toks, out_rows:] = jnp.where(first, low, 0.0).T.astype(BF16)
            select[n, toks:, :out_rows] = jnp.where(band & second, chosen, 0.0).T.astype(BF16)
            select[n, toks:, out_rows:] = jnp.zeros((toks, out_rows), BF16)
            n += 1

    def place(f, b, turned):
        count = 2 * 16 * f.slots
        shape = (16 * ROWS, count) if turned else (count, 16 * ROWS)
        out, src = iota(shape, int(turned)), iota(shape, 1 - int(turned))
        kind = (out >= count // 2).astype(jnp.int32)
        slot = out - kind * (count // 2)
        from_row = (slot // f.slots) * ROWS + slot % f.slots + kind * f.slots + b * f.height
        return (src == from_row).astype(BF16)

    def activate(rows, p, sums):
        gate, up, back_grad = (sums[:, n * piece : (n + 1) * piece] for n in range(3))
        sig = jax.nn.sigmoid(gate)
        smooth = gate * sig
        slope = sig * (1.0 + gate * (1.0 - sig))
        act_ref[core, p, rows, :piece] = (smooth * up).astype(BF16)
        act_ref[core, p, rows, piece : 2 * piece] = (back_grad * up * slope).astype(BF16)
        act_ref[core, p, rows, 2 * piece :] = (back_grad * smooth).astype(BF16)

    def units_of(side, p):
        return pl.ds(pl.multiple_of(side * half + p * piece, piece), piece)

    def project(x, d, side, p):
        return dot(x, pair_w[side * PIECES + p]), dot(d, down_t[:, units_of(side, p)])

    def work(part, beside_sums, beside_acts):
        f = form[part]
        rows = pl.ds(f.first * total, f.slots * total)
        group_rows = 16 * f.slots
        own_in(part).wait()
        wait_blocks(part, r1_sem)
        places = [place(f, b, False) for b in range(f.bands)]
        for g in range(total // 16):
            block = recv1[part][pl.ds(g * 16, 16)].reshape(16 * ROWS, f.cols * LANES)
            at = pl.ds(f.first * total + g * group_rows, group_rows)
            for b, (start, count) in enumerate(f.spans):
                value = dot(places[b], tile_cols(block, 0, count)).astype(BF16)
                span = pl.ds(start * LANES, count * LANES)
                x_ref[at, span] = value[:group_rows]
                d_ref[at, span] = value[group_rows:]

        x, d = x_ref[rows, :], d_ref[rows, :]
        to_pair, to_y, to_act, sums = [], [], [], []
        for p in range(PIECES):
            ahead, behind = project(x, d, 1 - core, p)
            pair_send[p, rows, : 2 * piece] = ahead
            pair_send[p, rows, 2 * piece :] = behind
            to_pair.append(
                pltpu.make_async_remote_copy(
                    src_ref=pair_send.at[p, rows],
                    dst_ref=pair_recv.at[p, rows],
                    send_sem=ps_sem.at[part, p],
                    recv_sem=pr_sem.at[part, p],
                    device_id=sibling,
                    device_id_type=MESH,
                )
            )
            to_pair[-1].start()
            mine = jnp.concatenate(project(x, d, core, p), axis=1)
            to_pair[p].wait_recv()
            mine = mine + pair_recv[p, rows]
            sums.append(mine)
            y_send[p, rows] = mine.astype(BF16)
            to_y.append([])
            for q in range(1, y_size):
                to_y[-1].append(
                    pltpu.make_async_remote_copy(
                        src_ref=y_send.at[p, rows],
                        dst_ref=y_recv.at[q - 1, p, rows],
                        send_sem=ys_sem.at[part, p, q - 1],
                        recv_sem=yr_sem.at[part, p, q - 1],
                        device_id={"ctx": ctx, "head": ((y + q) % y_size) * cores + core},
                        device_id_type=MESH,
                    )
                )
                to_y[-1][-1].start()
        send_quarters(*beside_sums)
        for p in range(PIECES):
            mine = sums[p]
            for q, copy in enumerate(to_y[p]):
                copy.wait_recv()
                mine = mine + y_recv[q, p, rows].astype(F32)
            activate(rows, p, mine)
            to_act.append(
                pltpu.make_async_remote_copy(
                    src_ref=act_ref.at[core, p, rows],
                    dst_ref=act_ref.at[core, p, rows],
                    send_sem=as_sem.at[part, p],
                    recv_sem=ar_sem.at[part, p],
                    device_id=sibling,
                    device_id_type=MESH,
                )
            )
            to_act[-1].start()
        send_quarters(*beside_acts)

        out, grad = 0.0, 0.0
        for far in range(2):
            side = 1 - core if far else core
            for p in range(PIECES):
                if far:
                    to_act[p].wait_recv()
                units = units_of(side, p)
                out += dot(act_ref[side, p, rows, :piece], down_w[units, :])
                grad += dot(act_ref[side, p, rows, piece:], pair_t[side * PIECES + p])
        out, grad = out.astype(BF16), grad.astype(BF16)
        places = [place(f, b, True) for b in range(f.bands)]
        for g in range(total // 16):
            at = slice(g * group_rows, (g + 1) * group_rows)
            both = jnp.concatenate([out[at], grad[at]], axis=0)
            block = 0.0
            for b, (start, count) in enumerate(f.spans):
                band = dot(places[b], tile_cols(both, start, count))
                if count < f.cols:
                    gap = jnp.zeros((16 * ROWS, (f.cols - count) * LANES), F32)
                    band = jnp.concatenate([band, gap], axis=1)
                block += band
            send2[part][pl.ds(g * 16 // heads, 16 // heads)] = block.astype(BF16).reshape(
                (16 // heads, heads) + f.block
            )
        return to_pair + sum(to_y, []) + to_act

    started = work(0, (1, False, (3,)), (1, False, ()))
    send_quarters(0, True, (0, 1))
    started += work(1, (0, True, (2,)), (0, True, (3,)))
    send_quarters(1, True, range(4))

    xt_ref[...] = x_ref[...].T
    for side in range(2):
        for p in range(PIECES):
            start = side * half + p * piece
            hidt_ref[start : start + piece, :] = act_ref[side, p, :, :piece].T
    out_copies = local(
        (
            (xt_ref, xt_hbm), (d_ref, d_hbm), (act_ref, act_hbm), (hidt_ref, hidt_hbm),
            (select, select_hbm),
        ),
        o_sem,
    )
    for copy in out_copies:
        copy.start()
    for copy in started:
        copy.wait_send()
    for part in range(PARTS):
        wait_blocks(part, s1_sem)
        wait_blocks(part, s2_sem)
        own_back(part).wait()
    for copy in out_copies:
        copy.wait()
    for part in range(PARTS):
        wait_blocks(part, r2_sem)


def finish_kernel(
    experts,
    routes_ref, dy_ref, back0_ref, back1_ref, xt_ref, d_ref, act_ref, hidt_ref, select,
    moe_ref, grad_tok_ref, grad_route_ref, gate_ref, up_ref, down_ref,
    inner,
):
    step = pl.program_id(0)
    picks, toks = routes_ref.shape
    slice_width = dy_ref.shape[1]
    width = experts * ROWS

    @pl.when(step == 0)
    def _():
        inner[...] = jnp.zeros_like(inner)

    count = down_ref.shape[0]
    piece = act_ref.shape[3] // 3
    piece_steps = piece // count
    slab, offset = step // piece_steps, (step % piece_steps) * count

    def units(start):
        at = pl.ds(pl.multiple_of(start * piece + offset, count), count)
        return act_ref[slab // PIECES, slab % PIECES, :, at]

    pair = dot(xt_ref[...], jnp.concatenate([units(1), units(2)], axis=1)).astype(BF16)
    gate_ref[...] = pair[:, :count]
    up_ref[...] = pair[:, count:]
    down_ref[...] = dot(hidt_ref[...], d_ref[...]).astype(BF16)

    combined, n = 0.0, 0
    for f, back_ref in zip(forms(slice_width), (back0_ref, back1_ref)):
        block = back_ref[:, 0].reshape(width, f.cols * LANES)
        twice = jnp.concatenate([block, block], axis=0)
        bands = []
        for start, count in f.spans:
            bands.append(dot(select[n], tile_cols(twice, 0, count)))
            span = slice(start * LANES, (start + count) * LANES)
            inner[n] += dot_nt(dy_ref[:, span], tile_cols(block, 0, count))
            n += 1
        combined += jnp.concatenate(bands, axis=1)
    moe_ref[...] = combined[:toks].astype(BF16)
    grad_tok_ref[...] = combined[toks:].astype(BF16)

    @pl.when(step == pl.num_programs(0) - 1)
    def _():
        found = 0.0
        for n in range(inner.shape[0]):
            chosen = select[n, :toks, :width].astype(F32) > 0.0
            found += jnp.where(chosen, inner[n], 0.0)
        found = found.T
        row_expert = iota((width, 1), 0) // ROWS
        for k in range(picks):
            grad_route_ref[k : k + 1, :] = jnp.sum(
                jnp.where(routes_ref[k : k + 1, :] == row_expert, found, 0.0), axis=0, keepdims=True
            )


def on_device(tokens, routes, route_weight, w_gate, w_up, w_down, grad_out):
    experts = lax.axis_size("ctx")
    heads = lax.axis_size("head")
    total = experts * heads
    toks, model_width = tokens.shape
    picks = routes.shape[1]
    slice_width, hidden = w_gate.shape[1:]
    all_rows = CAP * total
    y_others = max(1, heads // 2 - 1)
    piece = hidden // 2 // PIECES
    slots = experts * ROWS
    form = forms(slice_width)
    bands = sum(f.bands for f in form)
    vmem = pl.BlockSpec(memory_space=pltpu.VMEM)
    hbm = pl.BlockSpec(memory_space=pl.ANY)
    dma = pltpu.SemaphoreType.DMA
    handed = (
        (slice_width, all_rows),
        (all_rows, slice_width),
        (2, PIECES, all_rows, 3 * piece),
        (hidden, all_rows),
        (bands, 2 * toks, 2 * slots),
    )
    sums = (PIECES, all_rows, 3 * piece)
    xt, d_rows, acts, hidt, select, *back = pl.pallas_call(
        functools.partial(exchange_kernel, experts, heads),
        out_shape=tuple(
            jax.ShapeDtypeStruct(shape, BF16)
            for shape in handed + tuple((total,) + f.block for f in form)
        ),
        in_specs=[hbm] * 2 + [vmem] * 2 + [hbm] * 3,
        out_specs=(hbm,) * 7,
        scratch_shapes=[
            pltpu.VMEM((toks, model_width), BF16),
            pltpu.VMEM((toks, model_width), BF16),
            pltpu.VMEM((2 * PIECES, slice_width, 2 * piece), BF16),
            pltpu.VMEM((hidden, slice_width), BF16),
            pltpu.VMEM((2 * PIECES, 2 * piece, slice_width), BF16),
            pltpu.VMEM((slice_width, hidden), BF16),
            pltpu.VMEM(handed[1], BF16),
            pltpu.VMEM(handed[1], BF16),
            pltpu.VMEM(handed[2], BF16),
            pltpu.VMEM(handed[0], BF16),
            pltpu.VMEM(handed[3], BF16),
            pltpu.VMEM(handed[4], BF16),
            *(pltpu.VMEM((heads, experts) + f.block, BF16) for f in form),
            *(pltpu.VMEM((total,) + f.block, BF16) for f in form),
            *(pltpu.VMEM((experts, heads) + f.block, BF16) for f in form),
            pltpu.VMEM(sums, F32),
            pltpu.VMEM(sums, F32),
            pltpu.VMEM(sums, BF16),
            pltpu.VMEM((y_others,) + sums, BF16),
            dma((2,)),
            dma((1 + 4 * PIECES,)),
            dma((5,)),
            dma((2 * PARTS,)),
            dma((PARTS,)),
            dma((PARTS,)),
            dma((PARTS,)),
            dma((PARTS,)),
            dma((PARTS, PIECES)),
            dma((PARTS, PIECES)),
            dma((PARTS, PIECES, y_others)),
            dma((PARTS, PIECES, y_others)),
            dma((PARTS, PIECES)),
            dma((PARTS, PIECES)),
        ],
        compiler_params=pltpu.CompilerParams(
            collective_id=0, has_side_effects=True, vmem_limit_bytes=VMEM_BYTES
        ),
    )(tokens, grad_out, routes.T, route_weight.T, w_gate[0], w_up[0], w_down[0])

    back = [b.reshape((experts, heads) + f.block) for b, f in zip(back, form)]

    def whole(shape):
        return pl.BlockSpec(shape, lambda h: (0,) * len(shape))

    units = hidden // heads
    moe_out, grad_tokens, grad_route, grad_gate, grad_up, grad_down = pl.pallas_call(
        functools.partial(finish_kernel, experts),
        grid=(heads,),
        in_specs=[
            whole((picks, toks)),
            pl.BlockSpec((toks, slice_width), lambda h: (0, h)),
            *(pl.BlockSpec((experts, 1) + f.block, lambda h: (0, h, 0, 0)) for f in form),
            whole(handed[0]),
            whole(handed[1]),
            whole(handed[2]),
            pl.BlockSpec((units, all_rows), lambda h: (h, 0)),
            whole(handed[4]),
        ],
        out_specs=(
            pl.BlockSpec((toks, slice_width), lambda h: (0, h)),
            pl.BlockSpec((toks, slice_width), lambda h: (0, h)),
            whole((picks, toks)),
            pl.BlockSpec((slice_width, units), lambda h: (0, h)),
            pl.BlockSpec((slice_width, units), lambda h: (0, h)),
            pl.BlockSpec((units, slice_width), lambda h: (h, 0)),
        ),
        out_shape=(
            jax.ShapeDtypeStruct((toks, model_width), BF16),
            jax.ShapeDtypeStruct((toks, model_width), BF16),
            jax.ShapeDtypeStruct((picks, toks), F32),
            jax.ShapeDtypeStruct((slice_width, hidden), BF16),
            jax.ShapeDtypeStruct((slice_width, hidden), BF16),
            jax.ShapeDtypeStruct((hidden, slice_width), BF16),
        ),
        scratch_shapes=[pltpu.VMEM((bands, toks, slots), F32)],
        compiler_params=pltpu.CompilerParams(vmem_limit_bytes=VMEM_BYTES),
    )(routes.T, grad_out, *back, xt, d_rows, acts, hidt, select)
    return (moe_out, grad_tokens, grad_route.T, grad_gate[None], grad_up[None], grad_down[None])


def solution(mesh):
    tok = P(("ctx", "head"), None)
    col, row = P("ctx", "head", None), P("ctx", None, "head")
    return jax.shard_map(
        on_device,
        mesh=mesh,
        in_specs=(tok, tok, tok, col, col, row, tok),
        out_specs=(tok, tok, tok, col, col, row),
        check_vma=False,
    )
```
